32 devices in a mesh: groups: 2 (over y), seq: 4 (over z), head: 2 (over x), batch: 2 (over core).
Axes of the slice: x: 2, y: 2, z: 4, core: 2. Of those that a mesh axis runs over, the one named last changes fastest.
Arguments:
- x_values: bfloat16 [4, 1024, 8192], P(('groups', 'batch'), 'seq', 'head'), parts along dimension 0, may hold values from -6 to 6
- z_gate: bfloat16 [4, 1024, 8192], P(('groups', 'batch'), 'seq', 'head'), parts along dimension 0, may hold values from -6 to 6
- write_basis: bfloat16 [4, 1024, 1024], P(('groups', 'batch'), 'seq', 'head'), parts along dimension 0, may hold values from -6 to 6
- read_basis: bfloat16 [4, 1024, 1024], P(('groups', 'batch'), 'seq', 'head'), parts along dimension 0, may hold values from -0.5 to 0.5
- step_size: float32 [4, 1024, 128], P(('groups', 'batch'), 'seq', 'head'), parts along dimension 0, may hold values from 0.5 to 2
- log_decay: float32 [4, 1024, 128], P(('groups', 'batch'), 'seq', 'head'), parts along dimension 0, may hold values from -0.8 to 0
- cached_states: bfloat16 [4, 4, 128, 64, 128], P(('groups', 'batch'), None, 'head', 'seq'), parts along dimension 0, may hold values from -96 to 96
- session_slots: int32 [4, 4], P(('groups', 'batch')), parts along dimension 0, may hold values from 0 to 3, each once within a row
- conv_lengths: int32 [4, 4], P(('groups', 'batch')), parts along dimension 0, may hold values from 1 to 4, 8 in all within a row
- norm_gain: float32 [8192], P('head'), may hold values from 0.1 to 1.9
- out_weight: bfloat16 [8192, 4096], P('head', 'seq'), may hold values from -0.0625 to 0.0625
Outputs:
- layer_out: bfloat16 [4, 1024, 4096], P(('groups', 'batch'), 'seq', 'head'), parts along dimension 0
The draws below stay inside these ranges and needn't reach their ends.
There are 2 independent parts, one for each index of `groups`. The reference program is written for one: setup_inputs(seed, part) draws one part's arguments, and reference() takes and returns one part's arrays. A program takes and returns all parts, laid end to end along the dimension named above; an argument that names none is the same for every part. Nothing has to cross between parts.
Inputs may be any that keep to these rules, and one draw needn't show every extreme that they name: `session_slots`: each row's entries name every pool entry once. `conv_lengths`: each row's lengths sum to 8.
All inputs are finite; a program needn't handle non-finite values.
Results may differ from the reference program's by a relative error of at most 0.017.
Values may be sent and summed in bfloat16 or wider, within the bound.
No kernel may reach another device: no remote copies, remote signals or barrier semaphores. Data moves between devices by JAX's collectives and lax.ppermute only.
A program may use at most 128 MiB of HBM per device.

```python
import math
import jax
import jax.numpy as jnp
import numpy as np
from jax import lax

D = 4096
HEADS = 128
HEAD_DIM = 64
STATE = 128
GROUPS = 8
STRETCH = 128
CONVS = 4
BUNDLED_LINES = 2
LINE_SLOTS = 1024
STRETCHES_ROW = 8
MOST_STRETCHES = 4
N_HEAD = 2


def draw_log_decay(key, part):
    sampler_seeds = jax.random.split(key, 4)
    fading_speeds = jnp.exp(jax.random.uniform(sampler_seeds[0], (HEADS,), jnp.float32, math.log(0.5 / LINE_SLOTS), math.log(1.0 / 30.0)))
    shrink_multiplier = jnp.exp(jax.random.uniform(sampler_seeds[1], (BUNDLED_LINES, LINE_SLOTS, HEADS), jnp.float32, math.log(0.5), math.log(2.0)))
    word_spurts = jax.random.uniform(sampler_seeds[2], (BUNDLED_LINES, LINE_SLOTS, 1), jnp.float32) < 3.0 / LINE_SLOTS
    incoming_quantity = jax.random.uniform(sampler_seeds[3], (BUNDLED_LINES, LINE_SLOTS, HEADS), jnp.float32, 0.22, 0.69)
    return -(fading_speeds[None, None, :] * shrink_multiplier + jnp.where(word_spurts, incoming_quantity, 0.0))


def steps_of(stream_key, shape, pieces, low, high):
    factor_of, own = 1.0, jax.random.fold_in(stream_key, 6)
    for dim, blocks in pieces:
        steps = jnp.exp(jax.random.uniform(jax.random.fold_in(own, dim), (blocks,), jnp.float32, low / len(pieces), high / len(pieces)))
        factor_of = factor_of * jnp.repeat(steps, shape[dim] // blocks).reshape([-1 if axis == dim else 1 for axis in range(len(shape))])
    return factor_of


def length_profile(number_of, total, limit, slope):
    loads = [(1 << 20) // math.isqrt(standing ** slope) + 1 for standing in range(2, number_of + 1)]
    surplus, counts = total - limit - (number_of - 1), [1] * (number_of - 1)
    while surplus > 0:
        free = [i for i in range(number_of - 1) if counts[i] < limit]
        whole, budget = sum([loads[i] for i in free]), surplus
        for i in free:
            extra = min(limit - counts[i], max(1, budget * loads[i] // whole), surplus)
            counts[i] = counts[i] + extra
            surplus = surplus - extra
    return np.array([limit] + counts)


def uneven_parts(rng, number_of, total, most, lean):
    if number_of == 2:
        one = jax.random.randint(rng, (), max(1, total - most), min(most, total - 1) + 1)
        return jnp.stack([one, total - one])
    sizes = jnp.asarray(length_profile(number_of, total, most, lean), jnp.int32)
    twos = (number_of - 1) // 2
    source_of, sink = sizes[1:1 + 2 * twos:2], sizes[2:2 + 2 * twos:2]
    margin = jnp.minimum(source_of - 1, most - sink)
    shifted = jax.random.randint(jax.random.fold_in(rng, 1), (twos,), 0, 1 << 20) % (margin + 1)
    sizes = sizes.at[1:1 + 2 * twos:2].set(source_of - shifted).at[2:2 + 2 * twos:2].set(sink + shifted)
    return sizes[jax.random.permutation(jax.random.fold_in(rng, 2), number_of)]


def scatter_about(rng, dims, scale, limit, cuts=(), kind=jnp.bfloat16):
    factor_of = steps_of(rng, dims, cuts, -0.22, 0.18) if cuts else 1.0
    drawn = jax.random.normal(rng, dims, jnp.float32) * scale * factor_of
    return jnp.minimum(jnp.maximum(drawn, -limit), limit).astype(kind)


def setup_inputs(seed: int = 0, part: int = 0) -> dict:
    streams_of = jax.random.split(jax.random.key(seed), 12)
    part_splits = jax.random.split(jax.random.fold_in(streams_of[11], part), 12)
    x_values = scatter_about(part_splits[0], (BUNDLED_LINES, LINE_SLOTS, HEADS * HEAD_DIM), 1.0, 6.0, ((0, 2), (1, 4), (2, 2)))
    z_gate = scatter_about(part_splits[1], (BUNDLED_LINES, LINE_SLOTS, HEADS * HEAD_DIM), 1.0, 6.0, ((0, 2), (1, 4), (2, 2)))
    write_basis = scatter_about(part_splits[2], (BUNDLED_LINES, LINE_SLOTS, GROUPS * STATE), 1.0, 6.0, ((0, 2), (1, 4), (2, 2)))
    read_basis = scatter_about(part_splits[3], (BUNDLED_LINES, LINE_SLOTS, GROUPS * STATE), STATE ** -0.5, 0.5, ((0, 2), (1, 4), (2, 2)))
    step_size = jnp.clip(jnp.exp(math.log(2.0) - 1.3862944 * jax.random.uniform(part_splits[4], (BUNDLED_LINES, LINE_SLOTS, HEADS), jnp.float32) ** steps_of(part_splits[4], (BUNDLED_LINES, LINE_SLOTS, HEADS), ((0, 2), (1, 4), (2, 2)), -0.2, 0.2)), 0.5, 2.0)
    log_decay = draw_log_decay(jax.random.fold_in(jax.random.fold_in(streams_of[11], part), 71), part)
    cached_states = scatter_about(part_splits[6], (BUNDLED_LINES, CONVS, HEADS, HEAD_DIM, STATE), 16.0, 96.0, ((0, 2), (2, 2), (3, 4)))
    session_slots = jax.vmap(lambda own: jax.random.permutation(own, CONVS))(jax.random.split(part_splits[7], BUNDLED_LINES)).reshape((BUNDLED_LINES, CONVS)).astype(jnp.int32)
    conv_lengths = jax.vmap(lambda own: uneven_parts(own, CONVS, STRETCHES_ROW, MOST_STRETCHES, 2))(jax.random.split(part_splits[8], BUNDLED_LINES)).reshape((BUNDLED_LINES, CONVS)).astype(jnp.int32)
    norm_gain = jnp.clip(1.0 + 0.18 * jax.random.normal(streams_of[9], (HEADS * HEAD_DIM,), jnp.float32), 0.1, 1.9)
    out_weight = scatter_about(streams_of[10], (HEADS * HEAD_DIM, D), (HEADS * HEAD_DIM) ** -0.5, 0.0625, ((0, 2), (1, 4)))
    return {"x_values": x_values, "z_gate": z_gate, "write_basis": write_basis, "read_basis": read_basis, "step_size": step_size, "log_decay": log_decay, "cached_states": cached_states, "session_slots": session_slots, "conv_lengths": conv_lengths, "norm_gain": norm_gain, "out_weight": out_weight}


def row_states(x_row, write_row, read_row, step_row, decay_row, cached_row, slots_row, lengths_row):
    per_group = HEADS // GROUPS
    blocks = LINE_SLOTS // STRETCH
    begins = (jnp.cumsum(lengths_row) - lengths_row).astype(jnp.int32)
    block_ids = jnp.arange(blocks, dtype=jnp.int32)
    flags = jnp.any(begins[None, :] == block_ids[:, None], axis=1)
    owners = lax.optimization_barrier(jnp.sum((begins[None, :] <= block_ids[:, None]).astype(jnp.int32), axis=1)) - 1
    convs = jnp.arange(CONVS, dtype=jnp.int32)
    slot_ids = lax.optimization_barrier(jnp.sum(jnp.where(convs[None, :] == owners[:, None], slots_row[None, :], 0), axis=1)).astype(jnp.int32)
    values = x_row.reshape(blocks, STRETCH, HEADS, HEAD_DIM)
    writes = write_row.reshape(blocks, STRETCH, GROUPS, STATE)
    reads = read_row.reshape(blocks, STRETCH, GROUPS, STATE)
    steps_b = step_row.reshape(blocks, STRETCH, HEADS)
    logs = decay_row.reshape(blocks, STRETCH, HEADS)
    lower = jnp.arange(STRETCH)[:, None] >= jnp.arange(STRETCH)[None, :]

    def advance(state_now, item):
        value_b, write_b, read_b, step_b, log_b, flag, slot = item
        prior = lax.dynamic_index_in_dim(cached_row, slot, 0, keepdims=False).astype(jnp.float32)
        state_now = jnp.where(flag, prior, state_now)
        running = jnp.cumsum(log_b, axis=0)
        by_head = running.T
        spread = by_head[:, :, None] - by_head[:, None, :]
        fading = jnp.where(lower, jnp.exp(jnp.where(lower, spread, 0.0)), 0.0)
        scores = jnp.einsum('ign,jgn->gij', read_b.astype(jnp.float32), write_b.astype(jnp.float32))
        scores = jnp.repeat(scores, per_group, axis=0)
        mixing = (scores * fading * step_b.T[:, None, :]).astype(jnp.bfloat16)
        inner = jnp.einsum('hij,jhp->ihp', mixing.astype(jnp.float32), value_b.astype(jnp.float32))
        read_heads = jnp.repeat(read_b, per_group, axis=1).astype(jnp.float32)
        inflow = jnp.exp(running)[:, :, None] * jnp.einsum('ihn,hpn->ihp', read_heads, state_now, precision=lax.Precision.HIGHEST)
        write_heads = jnp.repeat(write_b, per_group, axis=1).astype(jnp.float32)
        to_end = jnp.exp(running[-1][None, :] - running) * step_b
        weighted = (write_heads * to_end[:, :, None]).astype(jnp.bfloat16)
        stretch_state = jnp.einsum('jhp,jhn->hpn', value_b.astype(jnp.float32), weighted.astype(jnp.float32))
        state_next = jnp.exp(running[-1])[:, None, None] * state_now + stretch_state
        return (state_next, inner + inflow)
    start_state = jnp.zeros((HEADS, HEAD_DIM, STATE), jnp.float32)
    unused, mixed = lax.scan(advance, start_state, (values, writes, reads, steps_b, logs, flags, slot_ids))
    return mixed.reshape(LINE_SLOTS, HEADS * HEAD_DIM)

def reference(x_values, z_gate, write_basis, read_basis, step_size, log_decay, cached_states, session_slots, conv_lengths, norm_gain, out_weight):
    outputs = []
    block_width = HEADS * HEAD_DIM // N_HEAD
    for row in range(BUNDLED_LINES):
        mixed = row_states(x_values[row], write_basis[row], read_basis[row], step_size[row], log_decay[row], cached_states[row], session_slots[row], conv_lengths[row])
        gated = mixed * jax.nn.silu(z_gate[row].astype(jnp.float32))
        grouped = gated.reshape(LINE_SLOTS, GROUPS, -1)
        scaled = grouped * lax.rsqrt(lax.optimization_barrier(jnp.mean(grouped * grouped, axis=2, keepdims=True)) + 1e-05)
        normed = (scaled.reshape(LINE_SLOTS, HEADS * HEAD_DIM) * norm_gain).astype(jnp.bfloat16)
        total = jnp.zeros((LINE_SLOTS, D), jnp.float32)
        for block in range(N_HEAD):
            partial_value = jnp.dot(normed[:, block * block_width:(block + 1) * block_width], out_weight[block * block_width:(block + 1) * block_width], preferred_element_type=jnp.float32)
            rounded = lax.optimization_barrier(partial_value.astype(jnp.bfloat16))
            total = total + rounded.astype(jnp.float32)
        outputs.append(total.astype(jnp.bfloat16))
    return jnp.stack(outputs)
```

```python
import functools

import jax
import jax.numpy as jnp
from jax import lax
from jax.experimental import pallas as pl
from jax.experimental.pallas import tpu as pltpu
from jax.sharding import PartitionSpec as P

HEAD_DIM = 64
STATE = 128
STRETCH = 128
BF = jnp.bfloat16
F32 = jnp.float32
VMEM_LIMIT = 48 * 1024 * 1024


def widen(per_head, width):
    heads = per_head.shape[1]
    high = per_head.astype(BF)
    low = (per_head - high.astype(F32)).astype(BF)
    both = jnp.concatenate([high, low], axis=1)
    place = lax.broadcasted_iota(jnp.int32, (2 * heads, width), 0)
    lane = lax.broadcasted_iota(jnp.int32, (2 * heads, width), 1)
    place = jnp.where(place >= heads, place - heads, place)
    spread = jnp.where(place == lane // (width // heads), 1.0, 0.0).astype(BF)
    return jnp.dot(both, spread, preferred_element_type=F32)


def states_kernel(x_ref, b_ref, end_ref, out_ref):
    width = x_ref.shape[1]
    for c in range(out_ref.shape[0]):
        rows = pl.ds(c * STRETCH, STRETCH)
        scaled = (x_ref[rows, :].astype(F32) * widen(end_ref[0, rows, :], width)).astype(BF)
        out_ref[c] = lax.dot_general(
            scaled, b_ref[rows, :], (((0,), (0,)), ((), ())), preferred_element_type=F32
        )


def block_states_of(x, b, to_end, blocks):
    tokens, width = x.shape
    groups_dev = b.shape[1] // STATE
    per = width // groups_dev
    return pl.pallas_call(
        states_kernel,
        grid=(groups_dev,),
        in_specs=[
            pl.BlockSpec((tokens, per), lambda g: (0, g)),
            pl.BlockSpec((tokens, STATE), lambda g: (0, g)),
            pl.BlockSpec((1, tokens, to_end.shape[2]), lambda g: (g, 0, 0)),
        ],
        out_specs=pl.BlockSpec((blocks, per, STATE), lambda g: (0, g, 0)),
        out_shape=jax.ShapeDtypeStruct((blocks, width, STATE), F32),
        compiler_params=pltpu.CompilerParams(vmem_limit_bytes=VMEM_LIMIT),
        cost_estimate=pl.CostEstimate(
            flops=2 * tokens * width * STATE * 4, bytes_accessed=8 << 20, transcendentals=0
        ),
    )(x, b, to_end)


def mix_kernel(
    code_ref,
    total_ref,
    x_ref,
    z_ref,
    b_ref,
    c_ref,
    run_ref,
    run_t_ref,
    step_t_ref,
    gain_ref,
    carry_ref,
    late_ref,
    early_ref,
    own_ref,
    out_ref,
    state,
    mixed,
):
    block = pl.program_id(0)
    width = x_ref.shape[1]
    heads = run_ref.shape[2]

    @pl.when(block == 0)
    def _():
        @pl.when(code_ref[0] == 0)
        def _():
            state[...] = carry_ref[...].astype(F32)

        @pl.when(code_ref[0] == 1)
        def _():
            state[...] = late_ref[...].astype(F32)

        @pl.when(code_ref[0] == 2)
        def _():
            state[...] = early_ref[...].astype(F32)

    @pl.when(block > 0)
    def _():
        @pl.when(code_ref[1] == 1)
        def _():
            state[...] = late_ref[...].astype(F32)

        @pl.when(code_ref[1] == 0)
        def _():
            for h in range(heads):
                rows = pl.ds(h * HEAD_DIM, HEAD_DIM)
                state[rows, :] = total_ref[h] * state[rows, :] + own_ref[0, rows, :]

    read = c_ref[...]
    scores = lax.dot_general(
        read, b_ref[...], (((1,), (1,)), ((), ())), preferred_element_type=F32
    )
    running = run_ref[0]
    inflow = lax.dot_general(
        read, state[...].astype(BF), (((1,), (1,)), ((), ())), preferred_element_type=F32
    )
    mixed[...] = inflow * widen(jnp.exp(running), width)
    row = lax.broadcasted_iota(jnp.int32, (STRETCH, STRETCH), 0)
    col = lax.broadcasted_iota(jnp.int32, (STRETCH, STRETCH), 1)
    lower = row >= col
    lane = lax.broadcasted_iota(jnp.int32, (STRETCH, 2 * HEAD_DIM), 1)
    for pair in range(heads // 2):
        mixes = []
        for h in (2 * pair, 2 * pair + 1):
            spread = running[:, h : h + 1] - run_t_ref[0, h : h + 1, :]
            fading = jnp.exp(jnp.where(lower, spread, -1e30))
            mixes.append((scores * fading * step_t_ref[0, h : h + 1, :]).astype(BF))
        lanes = pl.ds(pair * 2 * HEAD_DIM, 2 * HEAD_DIM)
        two = x_ref[:, lanes]
        none = jnp.zeros_like(two)
        stacked = jnp.concatenate(
            [jnp.where(lane < HEAD_DIM, two, none), jnp.where(lane < HEAD_DIM, none, two)], axis=0
        )
        mixed[:, lanes] += jnp.dot(
            jnp.concatenate(mixes, axis=1), stacked, preferred_element_type=F32
        )
    gate = z_ref[...].astype(F32)
    gated = mixed[...] * (gate / (1.0 + jnp.exp(-gate)))
    scale = lax.rsqrt(jnp.mean(gated * gated, axis=1, keepdims=True) + 1e-05)
    out_ref[...] = (gated * scale * gain_ref[...]).astype(BF)


def mix_group(g, code, totals, x, z, b, c, run, run_t, step_t, gain, carry, late, early, own):
    tokens, width = x.shape
    groups_dev = b.shape[1] // STATE
    per = width // groups_dev
    heads = run.shape[2]
    smem = pl.BlockSpec(memory_space=pltpu.SMEM)
    states = pl.BlockSpec((per, STATE), lambda i: (g, 0))
    return pl.pallas_call(
        mix_kernel,
        grid=(tokens // STRETCH,),
        in_specs=[
            smem,
            smem,
            pl.BlockSpec((STRETCH, per), lambda i: (i, g)),
            pl.BlockSpec((STRETCH, per), lambda i: (i, g)),
            pl.BlockSpec((STRETCH, STATE), lambda i: (i, g)),
            pl.BlockSpec((STRETCH, STATE), lambda i: (i, g)),
            pl.BlockSpec((1, STRETCH, heads), lambda i: (g, i, 0)),
            pl.BlockSpec((1, heads, STRETCH), lambda i: (g, 0, i)),
            pl.BlockSpec((1, heads, STRETCH), lambda i: (g, 0, i)),
            pl.BlockSpec((1, per), lambda i: (0, g)),
            pl.BlockSpec((per, STATE), lambda i: (0, 0)),
            states,
            states,
            pl.BlockSpec((1, per, STATE), lambda i: (0, g, 0)),
        ],
        out_specs=pl.BlockSpec((STRETCH, per), lambda i: (i, 0)),
        out_shape=jax.ShapeDtypeStruct((tokens, per), BF),
        scratch_shapes=[pltpu.VMEM((per, STATE), F32), pltpu.VMEM((STRETCH, per), F32)],
        compiler_params=pltpu.CompilerParams(vmem_limit_bytes=VMEM_LIMIT),
        cost_estimate=pl.CostEstimate(
            flops=tokens * per * 2 * 1024, bytes_accessed=4 << 20, transcendentals=0
        ),
    )(code, totals, x, z, b, c, run, run_t, step_t, gain, carry, late, early, own)


def project_kernel(count, pick_ref, *refs):
    lhs = refs[:count]
    first, second, out_ref, weight, sem = refs[count:]

    @pl.when(pick_ref[0] == 0)
    def _():
        pltpu.make_async_copy(first, weight, sem).start()

    @pl.when(pick_ref[0] != 0)
    def _():
        pltpu.make_async_copy(second, weight, sem).start()

    pltpu.make_async_copy(first, weight, sem).wait()
    place = 0
    for r in range(4):
        total = None
        for g in range(count // 4):
            own = lhs[g * 4 + r][...]
            depth = own.shape[1]
            part = jnp.dot(
                own, weight[g * depth : (g + 1) * depth, :], preferred_element_type=F32
            )
            total = part if total is None else total + part
        out_ref[place : place + total.shape[0], :] = total.astype(BF)
        place += total.shape[0]


def project(pick, lhs, first, second):
    tokens = 4 * lhs[0].shape[0]
    cols = first.shape[1]
    whole = pl.BlockSpec(memory_space=pltpu.VMEM)
    hbm = pl.BlockSpec(memory_space=pl.ANY)
    return pl.pallas_call(
        functools.partial(project_kernel, len(lhs)),
        in_specs=[pl.BlockSpec(memory_space=pltpu.SMEM)] + [whole] * len(lhs) + [hbm, hbm],
        out_specs=whole,
        out_shape=jax.ShapeDtypeStruct((tokens, cols), BF),
        scratch_shapes=[pltpu.VMEM(first.shape, BF), pltpu.SemaphoreType.DMA],
        compiler_params=pltpu.CompilerParams(vmem_limit_bytes=VMEM_LIMIT),
        cost_estimate=pl.CostEstimate(
            flops=2 * tokens * first.shape[0] * cols, bytes_accessed=11 << 20, transcendentals=0
        ),
    )(pick, *lhs, first, second)


SWAP = [(0, 1), (1, 0)]


def fast_projection(normed, out_weight):
    seq = lax.axis_index("seq")
    head = lax.axis_index("head")
    y = lax.axis_index("groups")
    core = lax.axis_index("batch")
    quarter = out_weight.shape[1] // 4
    own = lax.dynamic_slice_in_dim(out_weight, (2 * y + core) * quarter, quarter, 1)
    one = lax.ppermute(own, "seq", [(0, 1), (1, 0), (2, 3), (3, 2)])
    two_mid = lax.ppermute(own, "seq", [(1, 2), (2, 1)])
    two_end = lax.ppermute(two_mid, "seq", [(1, 0), (2, 3)])
    three_mid = lax.ppermute(one, "seq", [(1, 2), (2, 1)])
    three_end = lax.ppermute(three_mid, "seq", [(1, 0), (2, 3)])

    lhs = []
    for part in normed:
        across = lax.ppermute(part, "groups", SWAP)
        other = lax.ppermute(part, "batch", SWAP)
        other_across = lax.ppermute(across, "batch", SWAP)
        lhs += [part, other, across, other_across]
    zero = jnp.zeros((1,), jnp.int32)
    is_mid = jnp.logical_or(seq == 1, seq == 2).astype(jnp.int32).reshape(1)
    partials = [
        project(zero, lhs, own, own),
        project(zero, lhs, one, one),
        project(is_mid, lhs, two_end, two_mid),
        project(is_mid, lhs, three_end, three_mid),
    ]
    tokens = normed[0].shape[0]
    rows = []
    for number, partial_value in enumerate(partials):
        late = number >= 2
        goal = [(s // 2 + (1 if late else 0)) % 2 for s in range(4)]
        to_goal = [(2 * s + 1 - goal[s], 2 * s + goal[s]) for s in range(4)]
        arrived = lax.ppermute(partial_value, ("seq", "head"), to_goal)
        total = (partial_value.astype(F32) + arrived.astype(F32)).astype(BF)
        total = total.reshape(4, tokens, quarter)
        ends = [2 * s + goal[s] for s in range(4)]
        cross_y = [(a * 8 + e, (1 - a) * 8 + e) for a in (0, 1) for e in ends]
        from_y = lax.ppermute(total[2:], ("groups", "seq", "head"), cross_y)
        cross_core = [(2 * e + a, 2 * e + 1 - a) for a in (0, 1) for e in ends]
        from_core = lax.ppermute(
            jnp.stack([total[1], from_y[1]]), ("seq", "head", "batch"), cross_core
        )
        rows.append((total[0], from_core[0], from_y[0], from_core[1]))
    is_early = head == seq // 2
    swapped = jnp.where(is_early, seq % 2 == 1, seq >= 2)
    first = [jnp.where(is_early, a, b) for a, b in zip(rows[0], rows[2])]
    second = [jnp.where(is_early, a, b) for a, b in zip(rows[1], rows[3])]
    low = [jnp.where(swapped, b, a) for a, b in zip(first, second)]
    high = [jnp.where(swapped, a, b) for a, b in zip(first, second)]
    pieces = []
    for part in (low, high):
        a, b, c, d = part
        p = [jnp.where(core == 0, a, b), jnp.where(core == 0, b, a)]
        q = [jnp.where(core == 0, c, d), jnp.where(core == 0, d, c)]
        pieces += [jnp.where(y == 0, v, w) for v, w in zip(p + q, q + p)]
    return jnp.concatenate(pieces, axis=1)[None]


def plain_projection(normed, out_weight):
    tokens = normed.shape[0]
    pairs = lax.axis_size("batch")
    batch_index = lax.axis_index("batch")
    part_cols = out_weight.shape[1] // pairs
    own_part = lax.dynamic_slice_in_dim(out_weight, batch_index * part_cols, part_cols, 1)
    both_rows = lax.all_gather(normed, "batch", axis=0, tiled=True)
    partial_value = jnp.dot(
        both_rows,
        lax.all_gather(own_part, "seq", axis=1, tiled=True),
        preferred_element_type=F32,
    )
    summed = lax.psum_scatter(partial_value.astype(BF), "head", scatter_dimension=1, tiled=True)
    spans = summed.shape[1] // part_cols
    sections = summed.reshape(pairs, tokens, spans, 1, part_cols)
    regrouped = lax.all_to_all(sections, "batch", split_axis=0, concat_axis=3, tiled=True)
    return regrouped.reshape(1, tokens, spans * pairs * part_cols)


def exchange_states(cached, wanted, seq, size):
    heads, part = cached.shape[1], cached.shape[2]
    pieces = []
    for offset in range(size):
        entry = lax.dynamic_index_in_dim(wanted, (seq + offset) % size, 0, False)
        piece = lax.dynamic_index_in_dim(cached, entry, 0, False)
        if offset:
            piece = lax.ppermute(piece, "seq", [(i, (i + offset) % size) for i in range(size)])
        pieces.append((piece, (seq - offset) % size))
    whole = jnp.zeros((heads, size, part, cached.shape[3]), cached.dtype)
    owner = jnp.arange(size)[None, :, None, None]
    for piece, source in pieces:
        whole = jnp.where(owner == source, piece[:, None], whole)
    return whole.reshape(heads * size * part, cached.shape[3])


def body(
    x_values,
    z_gate,
    write_basis,
    read_basis,
    step_size,
    log_decay,
    cached_states,
    session_slots,
    conv_lengths,
    norm_gain,
    out_weight,
):
    tokens = x_values.shape[1]
    width = x_values.shape[2]
    heads_dev = step_size.shape[2]
    groups_dev = write_basis.shape[2] // STATE
    per_group = heads_dev // groups_dev
    per = width // groups_dev
    blocks = tokens // STRETCH
    size = lax.axis_size("seq")
    seq = lax.axis_index("seq")
    assert blocks == 2

    lengths_row = conv_lengths[0]
    begins = jnp.cumsum(lengths_row) - lengths_row
    all_blocks = jnp.arange(size * blocks, dtype=jnp.int32)
    starts = jnp.any(begins[None, :] == all_blocks[:, None], axis=1)
    owners = jnp.sum((begins[None, :] <= all_blocks[:, None]).astype(jnp.int32), axis=1) - 1
    convs = jnp.arange(lengths_row.shape[0], dtype=jnp.int32)
    slot_ids = jnp.sum(
        jnp.where(convs[None, :] == owners[:, None], session_slots[0][None, :], 0), axis=1
    )
    starts2 = starts.reshape(size, 2)
    slots2 = slot_ids.reshape(size, 2)
    want_late = jnp.where(starts2[:, 1], slots2[:, 1], slots2[:, 0])
    want_early = slots2[:, 0]
    flags = lax.dynamic_index_in_dim(starts2, seq, 0, False)
    late = exchange_states(cached_states[0], want_late, seq, size)
    early = exchange_states(cached_states[0], want_early, seq, size)
    code = jnp.stack(
        [
            jnp.where(flags[0], jnp.where(flags[1], 2, 1), 0),
            jnp.where(flags[1], 1, 0),
        ]
    ).astype(jnp.int32)

    logs = log_decay[0].reshape(blocks, STRETCH, heads_dev)
    running = jnp.cumsum(logs, axis=1)
    totals = jnp.exp(running[:, -1, :])
    to_end = (jnp.exp(running[:, -1:, :] - running)).reshape(tokens, heads_dev) * step_size[0]
    run = running.reshape(tokens, groups_dev, per_group)
    by_group = jnp.transpose(run, (1, 0, 2))
    by_row = jnp.transpose(run, (1, 2, 0))
    step_t = jnp.transpose(step_size[0].reshape(tokens, groups_dev, per_group), (1, 2, 0))
    end_g = jnp.transpose(to_end.reshape(tokens, groups_dev, per_group), (1, 0, 2))

    x, z, b, c = x_values[0], z_gate[0], write_basis[0], read_basis[0]
    own = block_states_of(x, b, end_g, blocks)

    gain_out = jnp.where(jnp.any(flags), 0.0, totals[0] * totals[1])
    keep = jnp.where(flags[1], 0.0, 1.0)
    wide = (heads_dev, HEAD_DIM, STATE)
    prior = jnp.where(jnp.any(flags), late.reshape(wide).astype(F32), 0.0)
    from_late = jnp.where(flags[1], totals[1], totals[0] * totals[1])[:, None, None]
    end_state = (
        from_late * prior
        + (keep * totals[1])[:, None, None] * own[0].reshape(wide)
        + own[1].reshape(wide)
    ).reshape(groups_dev, per, STATE)
    gain_rows = jnp.repeat(gain_out, HEAD_DIM).reshape(groups_dev, per, 1)

    gain = norm_gain.reshape(1, width)
    normed = []
    for g in range(groups_dev):
        carry = jnp.zeros((per, STATE), BF)
        for hop in range(size - 1):
            leaving = (gain_rows[g] * carry.astype(F32) + end_state[g]).astype(BF)
            carry = carry + lax.ppermute(leaving, "seq", [(hop, hop + 1)])
        heads = slice(g * per_group, (g + 1) * per_group)
        normed.append(
            mix_group(
                g, code, totals[0, heads], x, z, b, c, by_group, by_row, step_t, gain,
                carry, late, early, own,
            )
        )
    shared = lax.axis_size("groups") * lax.axis_size("batch")
    if size == 4 and lax.axis_size("head") == 2 and shared == 4 and out_weight.shape[1] == 1024:
        return fast_projection(normed, out_weight)
    return plain_projection(jnp.concatenate(normed, axis=1), out_weight)


def solution(mesh):
    placed = (
        P(("groups", "batch"), "seq", "head"),
        P(("groups", "batch"), "seq", "head"),
        P(("groups", "batch"), "seq", "head"),
        P(("groups", "batch"), "seq", "head"),
        P(("groups", "batch"), "seq", "head"),
        P(("groups", "batch"), "seq", "head"),
        P(("groups", "batch"), None, "head", "seq", None),
        P(("groups", "batch"), None),
        P(("groups", "batch"), None),
        P("head"),
        P("head", "seq"),
    )
    return jax.shard_map(
        body,
        mesh=mesh,
        in_specs=placed,
        out_specs=P(("groups", "batch"), "seq", "head"),
        check_vma=False,
    )
```

```python
import functools

import jax
import jax.numpy as jnp
from jax import lax
from jax.experimental import pallas as pl
from jax.experimental.pallas import tpu as pltpu
from jax.sharding import PartitionSpec as P

HEAD_DIM = 64
STATE = 128
STRETCH = 128
BF = jnp.bfloat16
F32 = jnp.float32
VMEM_LIMIT = 48 * 1024 * 1024
SMALL = pl.CostEstimate(flops=1000, bytes_accessed=1000, transcendentals=0)


def widen(per_head, width):
    heads = per_head.shape[1]
    high = per_head.astype(BF)
    low = (per_head - high.astype(F32)).astype(BF)
    both = jnp.concatenate([high, low], axis=1)
    place = lax.broadcasted_iota(jnp.int32, (2 * heads, width), 0)
    lane = lax.broadcasted_iota(jnp.int32, (2 * heads, width), 1)
    place = jnp.where(place >= heads, place - heads, place)
    spread = jnp.where(place == lane // (width // heads), 1.0, 0.0).astype(BF)
    return jnp.dot(both, spread, preferred_element_type=F32)


def states_kernel(x_ref, b_ref, end_ref, out_ref):
    width = x_ref.shape[1]
    for c in range(out_ref.shape[0]):
        rows = pl.ds(c * STRETCH, STRETCH)
        scaled = (x_ref[rows, :].astype(F32) * widen(end_ref[0, rows, :], width)).astype(BF)
        out_ref[c] = lax.dot_general(
            scaled, b_ref[rows, :], (((0,), (0,)), ((), ())), preferred_element_type=F32
        )


def block_states_of(x, b, to_end, blocks):
    tokens, width = x.shape
    groups_dev = b.shape[1] // STATE
    per = width // groups_dev
    return pl.pallas_call(
        states_kernel,
        grid=(groups_dev,),
        in_specs=[
            pl.BlockSpec((tokens, per), lambda g: (0, g)),
            pl.BlockSpec((tokens, STATE), lambda g: (0, g)),
            pl.BlockSpec((1, tokens, to_end.shape[2]), lambda g: (g, 0, 0)),
        ],
        out_specs=pl.BlockSpec((blocks, per, STATE), lambda g: (0, g, 0)),
        out_shape=jax.ShapeDtypeStruct((blocks, width, STATE), F32),
        compiler_params=pltpu.CompilerParams(vmem_limit_bytes=VMEM_LIMIT),
        cost_estimate=SMALL,
    )(x, b, to_end)


def pick_kernel(size, seq_ref, lengths_ref, slots_ref, cached, *refs):
    late, early, code_ref, sems = refs[:size], refs[size : 2 * size], refs[2 * size], refs[-1]
    convs = lengths_ref.shape[1]
    begins = [jnp.int32(0)]
    for j in range(convs - 1):
        begins.append(begins[-1] + lengths_ref[0, j])

    def starts(block):
        found = begins[0] == block
        for begin in begins[1:]:
            found = jnp.logical_or(found, begin == block)
        return found

    def slot(block):
        entry = slots_ref[0, 0]
        for j in range(1, convs):
            entry = jnp.where(begins[j] <= block, slots_ref[0, j], entry)
        return entry

    seq = seq_ref[0]
    copies = []
    for offset in range(size):
        target = seq + offset
        target = 2 * jnp.where(target >= size, target - size, target)
        last = jnp.where(starts(target + 1), slot(target + 1), slot(target))
        copies.append(pltpu.make_async_copy(cached.at[0, last], late[offset], sems.at[offset]))
        copies[-1].start()
        copies.append(
            pltpu.make_async_copy(cached.at[0, slot(target)], early[offset], sems.at[size + offset])
        )
        copies[-1].start()
    first = starts(2 * seq)
    second = starts(2 * seq + 1)
    code_ref[0] = jnp.where(first, jnp.where(second, 2, 1), 0).astype(jnp.int32)
    code_ref[1] = jnp.where(second, 1, 0).astype(jnp.int32)
    for copy in copies:
        copy.wait()


def pick_states(seq, lengths, slots, cached, size):
    smem = pl.BlockSpec(memory_space=pltpu.SMEM)
    hbm = pl.BlockSpec(memory_space=pl.ANY)
    piece = jax.ShapeDtypeStruct(cached.shape[2:], cached.dtype)
    out = pl.pallas_call(
        functools.partial(pick_kernel, size),
        in_specs=[smem, smem, smem, hbm],
        out_specs=[hbm] * (2 * size) + [smem],
        out_shape=[piece] * (2 * size) + [jax.ShapeDtypeStruct((2,), jnp.int32)],
        scratch_shapes=[pltpu.SemaphoreType.DMA((2 * size,))],
        cost_estimate=SMALL,
    )(seq.reshape(1), lengths, slots, cached)
    return out[:size], out[size : 2 * size], out[2 * size]


def end_kernel(code_ref, total_ref, late_ref, own_ref, out_ref):
    heads = out_ref.shape[0] // HEAD_DIM
    first = pl.program_id(0) * heads
    plain = jnp.logical_and(code_ref[0] == 0, code_ref[1] == 0)
    for h in range(heads):
        rows = pl.ds(h * HEAD_DIM, HEAD_DIM)
        gain0, gain1 = total_ref[0, first + h], total_ref[1, first + h]
        use_late = jnp.where(plain, 0.0, jnp.where(code_ref[1] == 1, gain1, gain0 * gain1))
        use_own = jnp.where(code_ref[1] == 1, 0.0, gain1)
        out_ref[rows, :] = (
            jnp.where(plain, 0.0, late_ref[rows, :].astype(F32) * use_late)
            + own_ref[0, rows, :] * use_own
            + own_ref[1, rows, :]
        )


def end_states(code, totals, late, own, per):
    width = late.shape[0]
    smem = pl.BlockSpec(memory_space=pltpu.SMEM)
    rows = pl.BlockSpec((per, STATE), lambda g: (g, 0))
    return pl.pallas_call(
        end_kernel,
        grid=(width // per,),
        in_specs=[smem, smem, rows, pl.BlockSpec((2, per, STATE), lambda g: (0, g, 0))],
        out_specs=rows,
        out_shape=jax.ShapeDtypeStruct((width, STATE), F32),
        cost_estimate=SMALL,
    )(code, totals, late, own)


def leave_kernel(place, code_ref, total_ref, carry_ref, end_ref, out_ref):
    heads = out_ref.shape[0] // HEAD_DIM
    first = (place + pl.program_id(0)) * heads
    passes = jnp.logical_and(code_ref[0] == 0, code_ref[1] == 0)
    for h in range(heads):
        rows = pl.ds(h * HEAD_DIM, HEAD_DIM)
        gain = jnp.where(passes, total_ref[0, first + h] * total_ref[1, first + h], 0.0)
        out_ref[rows, :] = (carry_ref[rows, :].astype(F32) * gain + end_ref[rows, :]).astype(BF)


def leaving_state(place, code, totals, carry, ends, per):
    smem = pl.BlockSpec(memory_space=pltpu.SMEM)
    rows = pl.BlockSpec((per, STATE), lambda g: (g, 0))
    return pl.pallas_call(
        functools.partial(leave_kernel, place),
        grid=(carry.shape[0] // per,),
        in_specs=[smem, smem, rows, pl.BlockSpec((per, STATE), lambda g: (place + g, 0))],
        out_specs=rows,
        out_shape=jax.ShapeDtypeStruct(carry.shape, BF),
        cost_estimate=SMALL,
    )(code, totals, carry, ends)


def mix_kernel(
    place,
    code_ref,
    total_ref,
    x_ref,
    z_ref,
    b_ref,
    c_ref,
    run_ref,
    run_t_ref,
    step_t_ref,
    gain_ref,
    carry_ref,
    late_ref,
    early_ref,
    own_ref,
    out_ref,
    state,
    mixed,
):
    block = pl.program_id(1)
    width = x_ref.shape[1]
    heads = run_ref.shape[2]
    head = (place + pl.program_id(0)) * heads

    @pl.when(block == 0)
    def _():
        @pl.when(code_ref[0] == 0)
        def _():
            state[...] = carry_ref[...].astype(F32)

        @pl.when(code_ref[0] == 1)
        def _():
            state[...] = late_ref[...].astype(F32)

        @pl.when(code_ref[0] == 2)
        def _():
            state[...] = early_ref[...].astype(F32)

    @pl.when(block > 0)
    def _():
        @pl.when(code_ref[1] == 1)
        def _():
            state[...] = late_ref[...].astype(F32)

        @pl.when(code_ref[1] == 0)
        def _():
            for h in range(heads):
                rows = pl.ds(h * HEAD_DIM, HEAD_DIM)
                state[rows, :] = total_ref[0, head + h] * state[rows, :] + own_ref[0, rows, :]

    read = c_ref[...]
    scores = lax.dot_general(
        read, b_ref[...], (((1,), (1,)), ((), ())), preferred_element_type=F32
    )
    running = run_ref[0]
    inflow = lax.dot_general(
        read, state[...].astype(BF), (((1,), (1,)), ((), ())), preferred_element_type=F32
    )
    mixed[...] = inflow * widen(jnp.exp(running), width)
    row = lax.broadcasted_iota(jnp.int32, (STRETCH, STRETCH), 0)
    col = lax.broadcasted_iota(jnp.int32, (STRETCH, STRETCH), 1)
    lower = row >= col
    lane = lax.broadcasted_iota(jnp.int32, (STRETCH, 2 * HEAD_DIM), 1)
    for pair in range(heads // 2):
        mixes = []
        for h in (2 * pair, 2 * pair + 1):
            spread = running[:, h : h + 1] - run_t_ref[0, h : h + 1, :]
            fading = jnp.exp(jnp.where(lower, spread, -1e30))
            mixes.append((scores * fading * step_t_ref[0, h : h + 1, :]).astype(BF))
        lanes = pl.ds(pair * 2 * HEAD_DIM, 2 * HEAD_DIM)
        two = x_ref[:, lanes]
        none = jnp.zeros_like(two)
        stacked = jnp.concatenate(
            [jnp.where(lane < HEAD_DIM, two, none), jnp.where(lane < HEAD_DIM, none, two)], axis=0
        )
        mixed[:, lanes] += jnp.dot(
            jnp.concatenate(mixes, axis=1), stacked, preferred_element_type=F32
        )
    gate = z_ref[...].astype(F32)
    gated = mixed[...] * (gate / (1.0 + jnp.exp(-gate)))
    scale = lax.rsqrt(jnp.mean(gated * gated, axis=1, keepdims=True) + 1e-05)
    out_ref[...] = (gated * scale * gain_ref[...]).astype(BF)


def mix_groups(place, count, code, totals, x, z, b, c, run, run_t, step_t, gain, carry, late, early, own):
    tokens, width = x.shape
    groups_dev = b.shape[1] // STATE
    per = width // groups_dev
    heads = run.shape[2]
    smem = pl.BlockSpec(memory_space=pltpu.SMEM)
    states = pl.BlockSpec((per, STATE), lambda g, i: (place + g, 0))
    wide = pl.BlockSpec((STRETCH, per), lambda g, i: (i, place + g))
    basis = pl.BlockSpec((STRETCH, STATE), lambda g, i: (i, place + g))
    rows = pl.BlockSpec((1, heads, STRETCH), lambda g, i: (place + g, 0, i))
    return pl.pallas_call(
        functools.partial(mix_kernel, place),
        grid=(count, tokens // STRETCH),
        in_specs=[
            smem,
            smem,
            wide,
            wide,
            basis,
            basis,
            pl.BlockSpec((1, STRETCH, heads), lambda g, i: (place + g, i, 0)),
            rows,
            rows,
            pl.BlockSpec((1, per), lambda g, i: (0, place + g)),
            pl.BlockSpec((per, STATE), lambda g, i: (g, 0)),
            states,
            states,
            pl.BlockSpec((1, per, STATE), lambda g, i: (0, place + g, 0)),
        ],
        out_specs=pl.BlockSpec((STRETCH, per), lambda g, i: (i, g)),
        out_shape=jax.ShapeDtypeStruct((tokens, count * per), BF),
        scratch_shapes=[pltpu.VMEM((per, STATE), F32), pltpu.VMEM((STRETCH, per), F32)],
        compiler_params=pltpu.CompilerParams(vmem_limit_bytes=VMEM_LIMIT),
        cost_estimate=SMALL,
    )(code, totals, x, z, b, c, run, run_t, step_t, gain, carry, late, early, own)


def project_kernel(count, picks, seq_ref, *refs):
    lhs = refs[: 4 * count]
    arrays = refs[4 * count : -3]
    out_ref, weight, sems = refs[-3:]
    depth = lhs[0].shape[1]
    cols = weight.shape[2]
    for n, block in enumerate(picks):
        for half, where in enumerate(block):
            for choice in sorted(set(where)):
                mine = [s for s, other in enumerate(where) if other == choice]
                hit = seq_ref[0] == mine[0]
                for s in mine[1:]:
                    hit = jnp.logical_or(hit, seq_ref[0] == s)

                @pl.when(hit)
                def _(n=n, half=half, choice=choice):
                    pltpu.make_async_copy(
                        arrays[choice[0]].at[pl.ds(choice[1], depth)],
                        weight.at[n, pl.ds(half * depth, depth)],
                        sems.at[n],
                    ).start()

    for n in range(len(picks)):
        pltpu.make_async_copy(weight.at[n], weight.at[n], sems.at[n]).wait()
        for r in range(4):
            total = None
            for half in range(count):
                part = jnp.dot(
                    lhs[4 * half + r][...],
                    weight[n, half * depth : (half + 1) * depth, :],
                    preferred_element_type=F32,
                )
                total = part if total is None else total + part
            rows = total.shape[0]
            out_ref[r * rows : (r + 1) * rows, n * cols : (n + 1) * cols] = total.astype(BF)


def project(seq, lhs, arrays, picks):
    count = len(lhs) // 4
    tokens = 4 * lhs[0].shape[0]
    cols = arrays[0].shape[1]
    depth = lhs[0].shape[1]
    whole = pl.BlockSpec(memory_space=pltpu.VMEM)
    hbm = pl.BlockSpec(memory_space=pl.ANY)
    return pl.pallas_call(
        functools.partial(project_kernel, count, picks),
        in_specs=[pl.BlockSpec(memory_space=pltpu.SMEM)]
        + [whole] * len(lhs)
        + [hbm] * len(arrays),
        out_specs=whole,
        out_shape=jax.ShapeDtypeStruct((tokens, len(picks) * cols), BF),
        scratch_shapes=[
            pltpu.VMEM((len(picks), count * depth, cols), BF),
            pltpu.SemaphoreType.DMA((len(picks),)),
        ],
        compiler_params=pltpu.CompilerParams(vmem_limit_bytes=VMEM_LIMIT),
        cost_estimate=SMALL,
    )(seq.reshape(1), *lhs, *arrays)


SWAP = [(0, 1), (1, 0)]


def after(value, *others):
    return lax.optimization_barrier((value, *others))[0]


def finish_fast(seq, head, y, core, early_sums, late_sums, tokens, quarter):
    is_early = head == seq // 2
    swapped = jnp.where(is_early, seq % 2 == 1, seq >= 2)
    first = [jnp.where(is_early, a, b) for a, b in zip(early_sums[0], late_sums[0])]
    second = [jnp.where(is_early, a, b) for a, b in zip(early_sums[1], late_sums[1])]
    low = [jnp.where(swapped, b, a) for a, b in zip(first, second)]
    high = [jnp.where(swapped, a, b) for a, b in zip(first, second)]
    pieces = []
    for part in (low, high):
        a, b, c, d = part
        p = [jnp.where(core == 0, a, b), jnp.where(core == 0, b, a)]
        q = [jnp.where(core == 0, c, d), jnp.where(core == 0, d, c)]
        pieces += [jnp.where(y == 0, v, w) for v, w in zip(p + q, q + p)]
    return jnp.concatenate(pieces, axis=1)[None]


def to_rows(partial_value, late, tokens):
    goal = [(s // 2 + (1 if late else 0)) % 2 for s in range(4)]
    to_goal = [(2 * s + 1 - goal[s], 2 * s + goal[s]) for s in range(4)]
    arrived = lax.ppermute(partial_value, ("seq", "head"), to_goal)
    total = (partial_value.astype(F32) + arrived.astype(F32)).astype(BF)
    total = total.reshape(4, tokens, total.shape[1])
    ends = [2 * s + goal[s] for s in range(4)]
    cross_y = [(a * 8 + e, (1 - a) * 8 + e) for a in (0, 1) for e in ends]
    from_y = lax.ppermute(total[2:], ("groups", "seq", "head"), cross_y)
    cross_core = [(2 * e + a, 2 * e + 1 - a) for a in (0, 1) for e in ends]
    from_core = lax.ppermute(
        jnp.stack([total[1], from_y[1]]), ("seq", "head", "batch"), cross_core
    )
    return total[0], from_core[0], from_y[0], from_core[1]


def plain_projection(normed, out_weight):
    tokens = normed.shape[0]
    pairs = lax.axis_size("batch")
    batch_index = lax.axis_index("batch")
    part_cols = out_weight.shape[1] // pairs
    own_part = lax.dynamic_slice_in_dim(out_weight, batch_index * part_cols, part_cols, 1)
    both_rows = lax.all_gather(normed, "batch", axis=0, tiled=True)
    partial_value = jnp.dot(
        both_rows,
        lax.all_gather(own_part, "seq", axis=1, tiled=True),
        preferred_element_type=F32,
    )
    summed = lax.psum_scatter(partial_value.astype(BF), "head", scatter_dimension=1, tiled=True)
    spans = summed.shape[1] // part_cols
    sections = summed.reshape(pairs, tokens, spans, 1, part_cols)
    regrouped = lax.all_to_all(sections, "batch", split_axis=0, concat_axis=3, tiled=True)
    return regrouped.reshape(1, tokens, spans * pairs * part_cols)


def exchange_states(payload, seq, size):
    heads, part, state = payload[0].shape
    whole = jnp.zeros((heads, size, part, state), payload[0].dtype)
    owner = jnp.arange(size)[None, :, None, None]
    for offset, piece in enumerate(payload):
        if offset:
            piece = lax.ppermute(piece, "seq", [(i, (i + offset) % size) for i in range(size)])
        whole = jnp.where(owner == (seq - offset) % size, piece[:, None], whole)
    return whole.reshape(heads * size * part, state)


def body(
    x_values,
    z_gate,
    write_basis,
    read_basis,
    step_size,
    log_decay,
    cached_states,
    session_slots,
    conv_lengths,
    norm_gain,
    out_weight,
):
    tokens = x_values.shape[1]
    width = x_values.shape[2]
    heads_dev = step_size.shape[2]
    groups_dev = write_basis.shape[2] // STATE
    per_group = heads_dev // groups_dev
    per = width // groups_dev
    blocks = tokens // STRETCH
    size = lax.axis_size("seq")
    seq = lax.axis_index("seq")
    assert blocks == 2

    shared = lax.axis_size("groups") * lax.axis_size("batch")
    fast = (
        size == 4
        and lax.axis_size("head") == 2
        and shared == 4
        and out_weight.shape == (4096, 1024)
        and groups_dev == 4
    )
    late_out, early_out, code = pick_states(
        seq, conv_lengths, session_slots, cached_states, size
    )
    late = exchange_states(late_out, seq, size)
    head = lax.axis_index("head")
    y = lax.axis_index("groups")
    core = lax.axis_index("batch")
    if fast:
        quarter = out_weight.shape[1] // 4
        half = out_weight.shape[0] // 2
        w_own = lax.dynamic_slice_in_dim(
            after(out_weight, code), (2 * y + core) * quarter, quarter, 1
        )
        w_side = lax.ppermute(w_own, "seq", [(1, 0), (3, 2), (2, 3)])
        w_mid = lax.ppermute(w_own, "seq", [(1, 2), (2, 1)])

    logs = log_decay[0].reshape(blocks, STRETCH, heads_dev)
    running = jnp.cumsum(logs, axis=1)
    totals = jnp.exp(running[:, -1, :])
    to_end = (jnp.exp(running[:, -1:, :] - running)).reshape(tokens, heads_dev) * step_size[0]
    run = running.reshape(tokens, groups_dev, per_group)
    by_group = jnp.transpose(run, (1, 0, 2))
    by_row = jnp.transpose(run, (1, 2, 0))
    step_t = jnp.transpose(step_size[0].reshape(tokens, groups_dev, per_group), (1, 2, 0))
    end_g = jnp.transpose(to_end.reshape(tokens, groups_dev, per_group), (1, 0, 2))

    x, z, b, c = x_values[0], z_gate[0], write_basis[0], read_basis[0]
    own = block_states_of(x, b, end_g, blocks)

    ends = end_states(code, totals, late, own, per)
    count = 2 if groups_dev % 2 == 0 else 1
    chunks = groups_dev // count
    span = count * per
    arrived = [[] for _ in range(chunks)]
    leaving = [ends[n * span : (n + 1) * span].astype(BF) for n in range(chunks)]
    early_out = [after(piece, leaving[0]) for piece in early_out]
    early = None
    for hop in range(size - 1):
        for n in range(chunks):
            if hop:
                leaving[n] = leaving_state(n * count, code, totals, arrived[n][-1], ends, per)
            arrived[n].append(lax.ppermute(leaving[n], "seq", [(hop, hop + 1)]))
        if early is None:
            early = exchange_states(early_out, seq, size)
        if fast and hop == 0:
            w_first = lax.ppermute(after(w_own, arrived[-1][0]), "seq", [(0, 1)])
        if fast and hop == 1:
            w_side, w_mid, arrived[0][1] = lax.optimization_barrier(
                (w_side, w_mid, arrived[0][1])
            )
            w_two = lax.ppermute(w_mid[:half], "seq", [(1, 0), (2, 3)])
            w_two_left = lax.ppermute(w_mid[half:], "seq", [(1, 0)])
            w_three_mid = lax.ppermute(w_side, "seq", [(2, 1)])
    if fast:
        w_two_right = lax.ppermute(after(w_mid[half:], arrived[-1][-1]), "seq", [(2, 3)])
        w_first, arrived[0][-1] = lax.optimization_barrier((w_first, arrived[0][-1]))
        w_first_mid = lax.ppermute(w_first, "seq", [(1, 2)])
        w_three_left = lax.ppermute(w_three_mid, "seq", [(1, 0)])
        w_three_right = lax.ppermute(w_first_mid, "seq", [(2, 3)])

    gain = norm_gain.reshape(1, width)
    normed = []
    for n in range(chunks):
        carry = functools.reduce(jnp.add, arrived[n])
        normed.append(
            mix_groups(
                n * count, count, code, totals, x, z, b, c, by_group, by_row, step_t, gain,
                carry, late, early, own,
            )
        )
    if not fast:
        return plain_projection(jnp.concatenate(normed, axis=1), out_weight)

    lhs = []
    for part in normed:
        across = lax.ppermute(part, "groups", SWAP)
        other = lax.ppermute(part, "batch", SWAP)
        other_across = lax.ppermute(across, "batch", SWAP)
        lhs += [part, other, across, other_across]
    one = project(
        seq,
        lhs,
        [w_own, w_side, w_first],
        [
            [[(0, 0)] * 4, [(0, half)] * 4],
            [[(1, 0), (2, 0), (1, 0), (1, 0)], [(1, half), (2, half), (1, half), (1, half)]],
        ],
    )
    two = project(
        seq,
        lhs,
        [w_two, w_two_left, w_two_right, w_mid],
        [[[(0, 0), (3, 0), (3, 0), (0, 0)], [(1, 0), (3, half), (3, half), (2, 0)]]],
    )
    arrays = [w_three_left, w_three_mid, w_first_mid, w_three_right]
    three = project(
        seq,
        lhs,
        arrays,
        [[[(s, 0) for s in range(4)], [(s, half) for s in range(4)]]],
    )
    sums = [to_rows(one, False, tokens), to_rows(two, True, tokens), to_rows(three, True, tokens)]
    early_sums = [[v[:, :quarter] for v in sums[0]], [v[:, quarter:] for v in sums[0]]]
    return finish_fast(seq, head, y, core, early_sums, sums[1:], tokens, quarter)


def solution(mesh):
    placed = (
        P(("groups", "batch"), "seq", "head"),
        P(("groups", "batch"), "seq", "head"),
        P(("groups", "batch"), "seq", "head"),
        P(("groups", "batch"), "seq", "head"),
        P(("groups", "batch"), "seq", "head"),
        P(("groups", "batch"), "seq", "head"),
        P(("groups", "batch"), None, "head", "seq", None),
        P(("groups", "batch"), None),
        P(("groups", "batch"), None),
        P("head"),
        P("head", "seq"),
    )
    return jax.shard_map(
        body,
        mesh=mesh,
        in_specs=placed,
        out_specs=P(("groups", "batch"), "seq", "head"),
        check_vma=False,
    )
```

```python
import functools

import jax
import jax.numpy as jnp
from jax import lax
from jax.experimental import pallas as pl
from jax.experimental.pallas import tpu as pltpu
from jax.sharding import PartitionSpec as P

HEAD_DIM = 64
STATE = 128
STRETCH = 128
PIECES = 2
BF = jnp.bfloat16
F32 = jnp.float32
VMEM_LIMIT = 56 * 1024 * 1024
SMALL = pl.CostEstimate(flops=1000, bytes_accessed=1000, transcendentals=0)


def widen(per_head, width):
    heads = per_head.shape[1]
    high = per_head.astype(BF)
    low = (per_head - high.astype(F32)).astype(BF)
    both = jnp.concatenate([high, low], axis=1)
    place = lax.broadcasted_iota(jnp.int32, (2 * heads, width), 0)
    lane = lax.broadcasted_iota(jnp.int32, (2 * heads, width), 1)
    place = jnp.where(place >= heads, place - heads, place)
    spread = jnp.where(place == lane // (width // heads), 1.0, 0.0).astype(BF)
    return jnp.dot(both, spread, preferred_element_type=F32)


def states_kernel(x_ref, b_ref, end_ref, out_ref):
    width = x_ref.shape[1]
    for c in range(out_ref.shape[0]):
        rows = pl.ds(c * STRETCH, STRETCH)
        scaled = (x_ref[rows, :].astype(F32) * widen(end_ref[0, rows, :], width)).astype(BF)
        out_ref[c] = lax.dot_general(
            scaled, b_ref[rows, :], (((0,), (0,)), ((), ())), preferred_element_type=F32
        )


def block_states_of(x, b, to_end, blocks):
    tokens, width = x.shape
    groups_dev = b.shape[1] // STATE
    per = width // groups_dev
    return pl.pallas_call(
        states_kernel,
        grid=(groups_dev,),
        in_specs=[
            pl.BlockSpec((tokens, per), lambda g: (0, g)),
            pl.BlockSpec((tokens, STATE), lambda g: (0, g)),
            pl.BlockSpec((1, tokens, to_end.shape[2]), lambda g: (g, 0, 0)),
        ],
        out_specs=pl.BlockSpec((blocks, per, STATE), lambda g: (0, g, 0)),
        out_shape=jax.ShapeDtypeStruct((blocks, width, STATE), F32),
        compiler_params=pltpu.CompilerParams(vmem_limit_bytes=VMEM_LIMIT),
        cost_estimate=pl.CostEstimate(
            flops=2 * tokens * width * STATE, bytes_accessed=16 << 20, transcendentals=0
        ),
    )(x, b, to_end)


def pick_kernel(size, seq_ref, lengths_ref, slots_ref, cached, *refs):
    late, early, code_ref, sems = refs[:size], refs[size : 2 * size], refs[2 * size], refs[-1]
    convs = lengths_ref.shape[1]
    begins = [jnp.int32(0)]
    for j in range(convs - 1):
        begins.append(begins[-1] + lengths_ref[0, j])

    def starts(block):
        found = begins[0] == block
        for begin in begins[1:]:
            found = jnp.logical_or(found, begin == block)
        return found

    def slot(block):
        entry = slots_ref[0, 0]
        for j in range(1, convs):
            entry = jnp.where(begins[j] <= block, slots_ref[0, j], entry)
        return entry

    seq = seq_ref[0]
    copies = []
    for offset in range(size):
        target = seq + offset
        target = 2 * jnp.where(target >= size, target - size, target)
        last = jnp.where(starts(target + 1), slot(target + 1), slot(target))
        copies.append(pltpu.make_async_copy(cached.at[0, last], late[offset], sems.at[offset]))
        copies[-1].start()
        copies.append(
            pltpu.make_async_copy(cached.at[0, slot(target)], early[offset], sems.at[size + offset])
        )
        copies[-1].start()
    first = starts(2 * seq)
    second = starts(2 * seq + 1)
    code_ref[0] = jnp.where(first, jnp.where(second, 2, 1), 0).astype(jnp.int32)
    code_ref[1] = jnp.where(second, 1, 0).astype(jnp.int32)
    for copy in copies:
        copy.wait()


def pick_states(seq, lengths, slots, cached, size):
    smem = pl.BlockSpec(memory_space=pltpu.SMEM)
    hbm = pl.BlockSpec(memory_space=pl.ANY)
    whole = pl.BlockSpec(memory_space=pltpu.VMEM)
    piece = jax.ShapeDtypeStruct(cached.shape[2:], cached.dtype)
    out = pl.pallas_call(
        functools.partial(pick_kernel, size),
        in_specs=[smem, smem, smem, hbm],
        out_specs=[whole] * (2 * size) + [smem],
        out_shape=[piece] * (2 * size) + [jax.ShapeDtypeStruct((2,), jnp.int32)],
        scratch_shapes=[pltpu.SemaphoreType.DMA((2 * size,))],
        cost_estimate=SMALL,
    )(seq.reshape(1), lengths, slots, cached)
    return out[:size], out[size : 2 * size], out[2 * size]


def gather_kernel(size, seq_ref, *refs):
    out_ref = refs[-1]
    part = refs[0].shape[1]
    for offset in range(size):
        source = seq_ref[0] - offset
        source = jnp.where(source < 0, source + size, source)
        out_ref[:, pl.ds(pl.multiple_of(source * part, part), part), :] = refs[offset][...]


def put_together(pieces, seq, size):
    heads, part, state = pieces[0].shape
    if part % 16 == 0:
        step = min(heads, 16)
        piece = pl.BlockSpec((step, part, state), lambda g: (g, 0, 0))
        whole = pl.pallas_call(
            functools.partial(gather_kernel, size),
            grid=(heads // step,),
            in_specs=[pl.BlockSpec(memory_space=pltpu.SMEM)] + [piece] * size,
            out_specs=pl.BlockSpec((step, size * part, state), lambda g: (g, 0, 0)),
            out_shape=jax.ShapeDtypeStruct((heads, size * part, state), pieces[0].dtype),
            compiler_params=pltpu.CompilerParams(vmem_limit_bytes=VMEM_LIMIT),
            cost_estimate=SMALL,
        )(seq.reshape(1), *pieces)
    else:
        whole = jnp.zeros((heads, size, part, state), pieces[0].dtype)
        owner = jnp.arange(size)[None, :, None, None]
        for offset, piece in enumerate(pieces):
            whole = jnp.where(owner == (seq - offset) % size, piece[:, None], whole)
    return whole.reshape(heads * size * part, state)


def end_kernel(size, seq_ref, code_ref, total_ref, own_ref, *refs):
    pieces, late_ref, end_ref = refs[:size], refs[size], refs[size + 1]
    leaves = refs[size + 2 :]
    group = pl.program_id(0)
    heads = end_ref.shape[0] // HEAD_DIM
    first = group * heads
    plain = jnp.logical_and(code_ref[0] == 0, code_ref[1] == 0)
    gather_kernel(size, seq_ref, *pieces, late_ref)
    for h in range(heads):
        rows = pl.ds(h * HEAD_DIM, HEAD_DIM)
        gain0, gain1 = total_ref[0, first + h], total_ref[1, first + h]
        use_late = jnp.where(plain, 0.0, jnp.where(code_ref[1] == 1, gain1, gain0 * gain1))
        use_own = jnp.where(code_ref[1] == 1, 0.0, gain1)
        end_ref[rows, :] = (
            jnp.where(plain, 0.0, late_ref[h].astype(F32) * use_late)
            + own_ref[0, rows, :] * use_own
            + own_ref[1, rows, :]
        )
    for n, leave_ref in enumerate(leaves):

        @pl.when(group == n)
        def _(leave_ref=leave_ref):
            leave_ref[...] = end_ref[...].astype(BF)


def end_states(seq, code, totals, pieces, own, per):
    size = len(pieces)
    heads_dev, part, state = pieces[0].shape
    width = own.shape[1]
    groups = width // per
    heads = heads_dev // groups
    if part % 16:
        pieces = [put_together(pieces, seq, size).reshape(heads_dev, size * part, state)]
        size, part = 1, size * part
        seq = jnp.zeros_like(seq)
    smem = pl.BlockSpec(memory_space=pltpu.SMEM)
    rows = pl.BlockSpec((per, STATE), lambda g: (g, 0))
    late, ends, *leaves = pl.pallas_call(
        functools.partial(end_kernel, size),
        grid=(groups,),
        in_specs=[smem, smem, smem, pl.BlockSpec((2, per, STATE), lambda g: (0, g, 0))]
        + [pl.BlockSpec((heads, part, state), lambda g: (g, 0, 0))] * size,
        out_specs=[pl.BlockSpec((heads, size * part, state), lambda g: (g, 0, 0)), rows]
        + [pl.BlockSpec((per, STATE), lambda g: (0, 0))] * groups,
        out_shape=[
            jax.ShapeDtypeStruct((heads_dev, size * part, state), BF),
            jax.ShapeDtypeStruct((width, STATE), F32),
        ]
        + [jax.ShapeDtypeStruct((per, STATE), BF)] * groups,
        compiler_params=pltpu.CompilerParams(vmem_limit_bytes=VMEM_LIMIT),
        cost_estimate=SMALL,
    )(seq.reshape(1), code, totals, own, *pieces)
    return late.reshape(width, state), ends, leaves


def leave_kernel(place, code_ref, total_ref, carry_ref, end_ref, out_ref):
    heads = out_ref.shape[0] // HEAD_DIM
    first = (place + pl.program_id(0)) * heads
    passes = jnp.logical_and(code_ref[0] == 0, code_ref[1] == 0)
    for h in range(heads):
        rows = pl.ds(h * HEAD_DIM, HEAD_DIM)
        gain = jnp.where(passes, total_ref[0, first + h] * total_ref[1, first + h], 0.0)
        out_ref[rows, :] = (carry_ref[rows, :].astype(F32) * gain + end_ref[rows, :]).astype(BF)


def leaving_state(place, code, totals, carry, ends, per):
    smem = pl.BlockSpec(memory_space=pltpu.SMEM)
    rows = pl.BlockSpec((per, STATE), lambda g: (g, 0))
    return pl.pallas_call(
        functools.partial(leave_kernel, place),
        grid=(carry.shape[0] // per,),
        in_specs=[smem, smem, rows, pl.BlockSpec((per, STATE), lambda g: (place + g, 0))],
        out_specs=rows,
        out_shape=jax.ShapeDtypeStruct(carry.shape, BF),
        compiler_params=pltpu.CompilerParams(vmem_limit_bytes=VMEM_LIMIT),
        cost_estimate=SMALL,
    )(code, totals, carry, ends)


def mix_kernel(
    place,
    code_ref,
    total_ref,
    x_ref,
    z_ref,
    b_ref,
    c_ref,
    run_ref,
    run_t_ref,
    step_t_ref,
    gain_ref,
    carry_ref,
    late_ref,
    early_ref,
    own_ref,
    out_ref,
    state,
    mixed,
):
    block = pl.program_id(1)
    width = x_ref.shape[1]
    heads = run_ref.shape[2]
    head = (place + pl.program_id(0)) * heads

    @pl.when(block == 0)
    def _():
        @pl.when(code_ref[0] == 0)
        def _():
            state[...] = carry_ref[...].astype(F32)

        @pl.when(code_ref[0] == 1)
        def _():
            state[...] = late_ref[...].astype(F32)

        @pl.when(code_ref[0] == 2)
        def _():
            state[...] = early_ref[...].astype(F32)

    @pl.when(block > 0)
    def _():
        @pl.when(code_ref[1] == 1)
        def _():
            state[...] = late_ref[...].astype(F32)

        @pl.when(code_ref[1] == 0)
        def _():
            for h in range(heads):
                rows = pl.ds(h * HEAD_DIM, HEAD_DIM)
                state[rows, :] = total_ref[0, head + h] * state[rows, :] + own_ref[0, rows, :]

    read = c_ref[...]
    scores = lax.dot_general(
        read, b_ref[...], (((1,), (1,)), ((), ())), preferred_element_type=F32
    )
    running = run_ref[0]
    inflow = lax.dot_general(
        read, state[...].astype(BF), (((1,), (1,)), ((), ())), preferred_element_type=F32
    )
    mixed[...] = inflow * widen(jnp.exp(running), width)
    row = lax.broadcasted_iota(jnp.int32, (STRETCH, STRETCH), 0)
    col = lax.broadcasted_iota(jnp.int32, (STRETCH, STRETCH), 1)
    lower = row >= col
    lane = lax.broadcasted_iota(jnp.int32, (STRETCH, 2 * HEAD_DIM), 1)
    for pair in range(heads // 2):
        mixes = []
        for h in (2 * pair, 2 * pair + 1):
            spread = running[:, h : h + 1] - run_t_ref[0, h : h + 1, :]
            fading = jnp.exp(jnp.where(lower, spread, -1e30))
            mixes.append((scores * fading * step_t_ref[0, h : h + 1, :]).astype(BF))
        lanes = pl.ds(pair * 2 * HEAD_DIM, 2 * HEAD_DIM)
        two = x_ref[:, lanes]
        none = jnp.zeros_like(two)
        stacked = jnp.concatenate(
            [jnp.where(lane < HEAD_DIM, two, none), jnp.where(lane < HEAD_DIM, none, two)], axis=0
        )
        mixed[:, lanes] += jnp.dot(
            jnp.concatenate(mixes, axis=1), stacked, preferred_element_type=F32
        )
    gate = z_ref[...].astype(F32)
    gated = mixed[...] * (gate / (1.0 + jnp.exp(-gate)))
    scale = lax.rsqrt(jnp.mean(gated * gated, axis=1, keepdims=True) + 1e-05)
    out_ref[...] = (gated * scale * gain_ref[...]).astype(BF)


def mix_groups(place, count, code, totals, x, z, b, c, run, run_t, step_t, gain, carry, late, early, own):
    tokens, width = x.shape
    groups_dev = b.shape[1] // STATE
    per = width // groups_dev
    heads = run.shape[2]
    smem = pl.BlockSpec(memory_space=pltpu.SMEM)
    states = pl.BlockSpec((per, STATE), lambda g, i: (place + g, 0))
    wide = pl.BlockSpec((STRETCH, per), lambda g, i: (i, place + g))
    basis = pl.BlockSpec((STRETCH, STATE), lambda g, i: (i, place + g))
    rows = pl.BlockSpec((1, heads, STRETCH), lambda g, i: (place + g, 0, i))
    return pl.pallas_call(
        functools.partial(mix_kernel, place),
        grid=(count, tokens // STRETCH),
        in_specs=[
            smem,
            smem,
            wide,
            wide,
            basis,
            basis,
            pl.BlockSpec((1, STRETCH, heads), lambda g, i: (place + g, i, 0)),
            rows,
            rows,
            pl.BlockSpec((1, per), lambda g, i: (0, place + g)),
            pl.BlockSpec((per, STATE), lambda g, i: (g, 0)),
            states,
            states,
            pl.BlockSpec((1, per, STATE), lambda g, i: (0, place + g, 0)),
        ],
        out_specs=pl.BlockSpec((STRETCH, per), lambda g, i: (i, g)),
        out_shape=jax.ShapeDtypeStruct((tokens, count * per), BF),
        scratch_shapes=[pltpu.VMEM((per, STATE), F32), pltpu.VMEM((STRETCH, per), F32)],
        compiler_params=pltpu.CompilerParams(vmem_limit_bytes=VMEM_LIMIT),
        cost_estimate=SMALL,
    )(code, totals, x, z, b, c, run, run_t, step_t, gain, carry, late, early, own)


def project_kernel(first_ref, *refs):
    weights, out_ref, rows_all, weight, total, sems = refs[-6:]
    lhs = refs[:-6]
    tokens, depth = lhs[0].shape
    cols = weights.shape[2]
    parts = len(lhs) // 4
    for part in range(parts):
        span = pl.ds(part * depth, depth)
        for r in range(4):
            pltpu.make_async_copy(
                lhs[4 * part + r],
                rows_all.at[part, pl.ds(r * tokens, tokens)],
                sems.at[0, part],
            ).start()
        for n in range(2):
            pltpu.make_async_copy(
                weights.at[first_ref[0] + n, span],
                weight.at[part, :, pl.ds(n * cols, cols)],
                sems.at[1, part],
            ).start()
    for part in range(parts):
        pltpu.make_async_copy(rows_all.at[part], rows_all.at[part], sems.at[0, part]).wait()
        pltpu.make_async_copy(weight.at[part], weight.at[part], sems.at[1, part]).wait()
        for r in range(4):
            span = pl.ds(r * tokens, tokens)
            product = jnp.dot(rows_all[part, span, :], weight[part], preferred_element_type=F32)
            if part == 0:
                total[span, :] = product
            elif part < parts - 1:
                total[span, :] += product
            else:
                out_ref[span, :] = (total[span, :] + product).astype(BF)


def project(first, lhs, weights):
    parts = len(lhs) // 4
    tokens = 4 * lhs[0].shape[0]
    depth, cols = weights.shape[1:]
    hbm = pl.BlockSpec(memory_space=pl.ANY)
    return pl.pallas_call(
        project_kernel,
        in_specs=[pl.BlockSpec(memory_space=pltpu.SMEM)] + [hbm] * (len(lhs) + 1),
        out_specs=pl.BlockSpec(memory_space=pltpu.VMEM),
        out_shape=jax.ShapeDtypeStruct((tokens, 2 * cols), BF),
        scratch_shapes=[
            pltpu.VMEM((parts, tokens, depth // parts), BF),
            pltpu.VMEM((parts, depth // parts, 2 * cols), BF),
            pltpu.VMEM((tokens, 2 * cols), F32),
            pltpu.SemaphoreType.DMA((2, parts)),
        ],
        compiler_params=pltpu.CompilerParams(vmem_limit_bytes=VMEM_LIMIT),
        cost_estimate=SMALL,
    )(first.reshape(1), *lhs, weights)


SWAP = [(0, 1), (1, 0)]


def after(value, *others):
    return lax.optimization_barrier((value, *others))[0]


def to_rows(own, others, tokens):
    arrived = lax.ppermute(others, "head", SWAP)
    total = (own.astype(F32) + arrived.astype(F32)).astype(BF)
    total = total.reshape(4, tokens, total.shape[1])
    from_y = lax.ppermute(total[2:], "groups", SWAP)
    from_core = lax.ppermute(jnp.stack([total[1], from_y[1]]), "batch", SWAP)
    return total[0], from_core[0], from_y[0], from_core[1]


def in_order(y, core, parts):
    a, b, c, d = parts
    p = [jnp.where(core == 0, a, b), jnp.where(core == 0, b, a)]
    q = [jnp.where(core == 0, c, d), jnp.where(core == 0, d, c)]
    return [jnp.where(y == 0, v, w) for v, w in zip(p + q, q + p)]


def plain_projection(normed, out_weight):
    tokens = normed.shape[0]
    pairs = lax.axis_size("batch")
    batch_index = lax.axis_index("batch")
    part_cols = out_weight.shape[1] // pairs
    own_part = lax.dynamic_slice_in_dim(out_weight, batch_index * part_cols, part_cols, 1)
    both_rows = lax.all_gather(normed, "batch", axis=0, tiled=True)
    partial_value = jnp.dot(
        both_rows,
        lax.all_gather(own_part, "seq", axis=1, tiled=True),
        preferred_element_type=F32,
    )
    summed = lax.psum_scatter(partial_value.astype(BF), "head", scatter_dimension=1, tiled=True)
    spans = summed.shape[1] // part_cols
    sections = summed.reshape(pairs, tokens, spans, 1, part_cols)
    regrouped = lax.all_to_all(sections, "batch", split_axis=0, concat_axis=3, tiled=True)
    return regrouped.reshape(1, tokens, spans * pairs * part_cols)


def exchange_states(payload, seq, size):
    return [
        lax.ppermute(piece, "seq", [(i, (i + offset) % size) for i in range(size)])
        if offset
        else piece
        for offset, piece in enumerate(payload)
    ]


def body(
    x_values,
    z_gate,
    write_basis,
    read_basis,
    step_size,
    log_decay,
    cached_states,
    session_slots,
    conv_lengths,
    norm_gain,
    out_weight,
):
    tokens = x_values.shape[1]
    width = x_values.shape[2]
    heads_dev = step_size.shape[2]
    groups_dev = write_basis.shape[2] // STATE
    per_group = heads_dev // groups_dev
    per = width // groups_dev
    blocks = tokens // STRETCH
    size = lax.axis_size("seq")
    seq = lax.axis_index("seq")
    assert blocks == 2

    shared = lax.axis_size("groups") * lax.axis_size("batch")
    fast = (
        size == 4
        and lax.axis_size("head") == 2
        and shared == 4
        and out_weight.shape == (4096, 1024)
        and groups_dev == 4
    )
    late_out, early_out, code = pick_states(
        seq, conv_lengths, session_slots, cached_states, size
    )
    late_pieces = exchange_states(late_out, seq, size)
    head = lax.axis_index("head")
    y = lax.axis_index("groups")
    core = lax.axis_index("batch")
    if fast:
        quarter = out_weight.shape[1] // 4
        piece = quarter // PIECES
        w_own = [
            lax.dynamic_slice_in_dim(
                out_weight, (2 * y + core) * quarter + k * piece, piece, 1
            )
            for k in range(PIECES)
        ]

    logs = log_decay[0].reshape(blocks, STRETCH, heads_dev)
    running = jnp.cumsum(logs, axis=1)
    totals = jnp.exp(running[:, -1, :])
    to_end = (jnp.exp(running[:, -1:, :] - running)).reshape(tokens, heads_dev) * step_size[0]
    run = running.reshape(tokens, groups_dev, per_group)
    by_group = jnp.transpose(run, (1, 0, 2))
    by_row = jnp.transpose(run, (1, 2, 0))
    step_t = jnp.transpose(step_size[0].reshape(tokens, groups_dev, per_group), (1, 2, 0))
    end_g = jnp.transpose(to_end.reshape(tokens, groups_dev, per_group), (1, 0, 2))

    x, z, b, c = x_values[0], z_gate[0], write_basis[0], read_basis[0]
    own = block_states_of(x, b, end_g, blocks)

    count = 1
    chunks = groups_dev // count
    arrived = [[] for _ in range(chunks)]
    late, ends, leaving = end_states(seq, code, totals, late_pieces, own, per)
    early_pieces = exchange_states([after(piece, own) for piece in early_out], seq, size)
    weights = None
    for hop in range(size - 1):
        for n in range(chunks):
            if hop:
                leaving[n] = leaving_state(
                    n * count, code, totals, arrived[n][-1], ends, per
                )
            arrived[n].append(lax.ppermute(leaving[n], "seq", [(hop, hop + 1)]))
        if fast and weights is None:
            weights = [
                lax.all_gather(after(part, arrived[0][0], *early_pieces), "seq", axis=0)
                for part in w_own
            ]
    early = put_together(early_pieces, seq, size)

    gain = norm_gain.reshape(1, width)
    normed = []
    for n in range(chunks):
        carry = functools.reduce(jnp.add, arrived[n])
        normed.append(
            mix_groups(
                n * count, count, code, totals, x, z, b, c, by_group, by_row, step_t, gain,
                carry, late, early, own,
            )
        )
    if not fast:
        return plain_projection(jnp.concatenate(normed, axis=1), out_weight)

    lhs = []
    for part in normed:
        across = lax.ppermute(part, "groups", SWAP)
        other = lax.ppermute(part, "batch", SWAP)
        other_across = lax.ppermute(across, "batch", SWAP)
        lhs += [part, other, across, other_across]
    sides = []
    for part in weights:
        others = project(2 - 2 * head, lhs, part)
        mine = project(2 * head, lhs, part)
        sides.append(in_order(y, core, to_rows(mine, others, tokens)))
    pieces = [
        sides[k][q][:, block * piece : (block + 1) * piece]
        for block in range(2)
        for q in range(4)
        for k in range(PIECES)
    ]
    return jnp.concatenate(pieces, axis=1)[None]


def solution(mesh):
    placed = (
        P(("groups", "batch"), "seq", "head"),
        P(("groups", "batch"), "seq", "head"),
        P(("groups", "batch"), "seq", "head"),
        P(("groups", "batch"), "seq", "head"),
        P(("groups", "batch"), "seq", "head"),
        P(("groups", "batch"), "seq", "head"),
        P(("groups", "batch"), None, "head", "seq", None),
        P(("groups", "batch"), None),
        P(("groups", "batch"), None),
        P("head"),
        P("head", "seq"),
    )
    return jax.shard_map(
        body,
        mesh=mesh,
        in_specs=placed,
        out_specs=P(("groups", "batch"), "seq", "head"),
        check_vma=False,
    )
```

```python
import functools

import jax
import jax.numpy as jnp
from jax import lax
from jax.experimental import pallas as pl
from jax.experimental.pallas import tpu as pltpu
from jax.sharding import PartitionSpec as P

HEAD_DIM = 64
STATE = 128
STRETCH = 128
PIECES = 2
BF = jnp.bfloat16
F32 = jnp.float32
VMEM_LIMIT = 56 * 1024 * 1024
SMALL = pl.CostEstimate(flops=1000, bytes_accessed=1000, transcendentals=0)


def widen(per_head, width):
    heads = per_head.shape[1]
    high = per_head.astype(BF)
    low = (per_head - high.astype(F32)).astype(BF)
    both = jnp.concatenate([high, low], axis=1)
    place = lax.broadcasted_iota(jnp.int32, (2 * heads, width), 0)
    lane = lax.broadcasted_iota(jnp.int32, (2 * heads, width), 1)
    place = jnp.where(place >= heads, place - heads, place)
    spread = jnp.where(place == lane // (width // heads), 1.0, 0.0).astype(BF)
    return jnp.dot(both, spread, preferred_element_type=F32)


def states_kernel(x_ref, b_ref, end_ref, out_ref):
    width = x_ref.shape[1]
    for c in range(out_ref.shape[0]):
        rows = pl.ds(c * STRETCH, STRETCH)
        scaled = (x_ref[rows, :].astype(F32) * widen(end_ref[0, rows, :], width)).astype(BF)
        out_ref[c] = lax.dot_general(
            scaled, b_ref[rows, :], (((0,), (0,)), ((), ())), preferred_element_type=F32
        )


def block_states_of(x, b, to_end, blocks):
    tokens, width = x.shape
    groups_dev = b.shape[1] // STATE
    per = width // groups_dev
    return pl.pallas_call(
        states_kernel,
        grid=(groups_dev,),
        in_specs=[
            pl.BlockSpec((tokens, per), lambda g: (0, g)),
            pl.BlockSpec((tokens, STATE), lambda g: (0, g)),
            pl.BlockSpec((1, tokens, to_end.shape[2]), lambda g: (g, 0, 0)),
        ],
        out_specs=pl.BlockSpec((blocks, per, STATE), lambda g: (0, g, 0)),
        out_shape=jax.ShapeDtypeStruct((blocks, width, STATE), F32),
        compiler_params=pltpu.CompilerParams(vmem_limit_bytes=VMEM_LIMIT),
        cost_estimate=pl.CostEstimate(
            flops=2 * tokens * width * STATE, bytes_accessed=16 << 20, transcendentals=0
        ),
    )(x, b, to_end)


def row_starts(lengths_ref, slots_ref):
    convs = lengths_ref.shape[1]
    begins = [jnp.int32(0)]
    for j in range(convs - 1):
        begins.append(begins[-1] + lengths_ref[0, j])

    def starts(block):
        found = begins[0] == block
        for begin in begins[1:]:
            found = jnp.logical_or(found, begin == block)
        return found

    def slot(block):
        entry = slots_ref[0, 0]
        for j in range(1, convs):
            entry = jnp.where(begins[j] <= block, slots_ref[0, j], entry)
        return entry

    return starts, slot


def along(seq, offset, size):
    place = seq + offset
    return jnp.where(place >= size, place - size, place)


def second_kernel(size, seq_ref, lengths_ref, slots_ref, cached, *refs):
    pieces, code_ref, sems = refs[:size], refs[size], refs[-1]
    starts, slot = row_starts(lengths_ref, slots_ref)
    seq = seq_ref[0]
    copies = []
    for offset in range(size):
        entry = slot(2 * along(seq, offset, size) + 1)
        copies.append(pltpu.make_async_copy(cached.at[0, entry], pieces[offset], sems.at[offset]))
        copies[-1].start()
    code_ref[0] = jnp.where(starts(2 * seq + 1), 1, 0).astype(jnp.int32)
    for copy in copies:
        copy.wait()


def second_states(seq, lengths, slots, cached, size):
    smem = pl.BlockSpec(memory_space=pltpu.SMEM)
    whole = pl.BlockSpec(memory_space=pltpu.VMEM)
    piece = jax.ShapeDtypeStruct(cached.shape[2:], cached.dtype)
    *pieces, code = pl.pallas_call(
        functools.partial(second_kernel, size),
        in_specs=[smem, smem, smem, pl.BlockSpec(memory_space=pl.ANY)],
        out_specs=[whole] * size + [smem],
        out_shape=[piece] * size + [jax.ShapeDtypeStruct((1,), jnp.int32)],
        scratch_shapes=[pltpu.SemaphoreType.DMA((size,))],
        cost_estimate=SMALL,
    )(seq.reshape(1), lengths, slots, cached)
    return pieces, code


def split_kernel(size, seq_ref, code_ref, total_ref, gain_ref, own_ref, *refs):
    pieces, added = refs[:size], refs[size]
    group = pl.program_id(0)
    per = own_ref.shape[1]
    heads = per // HEAD_DIM
    part = HEAD_DIM // size
    for h in range(heads):
        rows = pl.ds(h * HEAD_DIM, HEAD_DIM)
        gain = jnp.where(code_ref[0] == 1, 0.0, total_ref[1, group * heads + h])
        added[rows, :] = (own_ref[0, rows, :] * gain + own_ref[1, rows, :]).astype(BF)
    for d in range(size):
        start = along(seq_ref[0], d, size) * part
        for h in range(heads):
            rows = pl.ds(pl.multiple_of(h * HEAD_DIM + start, part), part)
            pieces[d][group * heads + h] = added[rows, :]

    @pl.when(group == 0)
    def _():
        for piece in pieces:
            piece[piece.shape[0] - 1] = gain_ref[...]


def split_states(seq, code, totals, gains, own, per, size):
    width = own.shape[1]
    heads_dev = width // HEAD_DIM
    smem = pl.BlockSpec(memory_space=pltpu.SMEM)
    whole = pl.BlockSpec(memory_space=pltpu.VMEM)
    shape = (heads_dev + 1, HEAD_DIM // size, STATE)
    return pl.pallas_call(
        functools.partial(split_kernel, size),
        grid=(width // per,),
        in_specs=[smem, smem, smem, whole, pl.BlockSpec((2, per, STATE), lambda g: (0, g, 0))],
        out_specs=[pl.BlockSpec(shape, lambda g: (0, 0, 0))] * size,
        out_shape=[jax.ShapeDtypeStruct(shape, BF)] * size,
        scratch_shapes=[pltpu.VMEM((per, STATE), BF)],
        compiler_params=pltpu.CompilerParams(vmem_limit_bytes=VMEM_LIMIT),
        cost_estimate=SMALL,
    )(seq.reshape(1), code, totals, gains, own)


def enter_kernel(size, seq_ref, lengths_ref, slots_ref, cached_ref, *refs):
    pieces, outs, added, entering = refs[:size], refs[size : 2 * size], refs[-2], refs[-1]
    starts, slot = row_starts(lengths_ref, slots_ref)
    seq = seq_ref[0]
    heads_dev = cached_ref.shape[2]
    for d in range(size):
        source = seq - d
        added[jnp.where(source < 0, source + size, source)] = pieces[d][...]
    for t in range(size):
        if t:
            second = starts(2 * t - 1)
            before = slot(2 * t - 1)
            first = starts(2 * t)

            @pl.when(first)
            def _(t=t):
                entering[t] = cached_ref[0, slot(2 * t)]

            @pl.when(jnp.logical_not(first))
            def _(t=t, second=second, before=before):
                high = added[t - 1, heads_dev].astype(F32)
                gains = high[0:1, :] + high[1:2, :]
                for h in range(heads_dev):
                    both = gains[:, h : h + 1]
                    last = gains[:, heads_dev + h : heads_dev + h + 1]
                    old = jnp.where(
                        second,
                        cached_ref[0, before, h].astype(F32) * last,
                        entering[t - 1, h].astype(F32) * both,
                    )
                    entering[t, h] = (old + added[t - 1, h].astype(F32)).astype(BF)

        else:
            entering[0] = cached_ref[0, slot(0)]
    for d in range(size):
        outs[d][...] = entering[along(seq, d, size)]


def entering_states(seq, lengths, slots, cached, pieces):
    size = len(pieces)
    shape = cached.shape[2:]
    smem = pl.BlockSpec(memory_space=pltpu.SMEM)
    whole = pl.BlockSpec(memory_space=pltpu.VMEM)
    return pl.pallas_call(
        functools.partial(enter_kernel, size),
        in_specs=[smem, smem, smem] + [whole] * (size + 1),
        out_specs=[whole] * size,
        out_shape=[jax.ShapeDtypeStruct(shape, BF)] * size,
        scratch_shapes=[
            pltpu.VMEM((size,) + pieces[0].shape, BF),
            pltpu.VMEM((size,) + shape, BF),
        ],
        compiler_params=pltpu.CompilerParams(vmem_limit_bytes=VMEM_LIMIT),
        cost_estimate=SMALL,
    )(seq.reshape(1), lengths, slots, cached, *pieces)


def plain_entering(seq, lengths, slots, cached, totals, own, size):
    heads_dev, part = cached.shape[2:4]
    begins = jnp.cumsum(lengths[0]) - lengths[0]
    blocks = jnp.arange(2 * size, dtype=jnp.int32)
    starts = jnp.any(begins[None, :] == blocks[:, None], axis=1)
    owners = jnp.sum((begins[None, :] <= blocks[:, None]).astype(jnp.int32), axis=1) - 1
    entries = jnp.take(cached[0], jnp.take(slots[0], owners), axis=0)
    second = lax.all_to_all(entries[1::2], "seq", 0, 0, tiled=True)
    code = lax.dynamic_index_in_dim(starts, 2 * seq + 1, 0, True).astype(jnp.int32)
    states = own.reshape(2, heads_dev, HEAD_DIM, STATE)
    keep = jnp.where(code[0] == 1, 0.0, totals[1])[:, None, None]
    added = (keep * states[0] + states[1]).astype(BF)
    added = jnp.transpose(added.reshape(heads_dev, size, part, STATE), (1, 0, 2, 3))
    added = lax.all_to_all(added, "seq", 0, 0, tiled=True)
    gains = lax.all_gather(totals, "seq")
    entering = [entries[0]]
    for t in range(1, size):
        last = gains[t - 1, 1][:, None, None]
        both = (gains[t - 1, 0] * gains[t - 1, 1])[:, None, None]
        old = jnp.where(
            starts[2 * t - 1],
            entries[2 * t - 1].astype(F32) * last,
            entering[-1].astype(F32) * both,
        )
        carry = (old + added[t - 1].astype(F32)).astype(BF)
        entering.append(jnp.where(starts[2 * t], entries[2 * t], carry))
    entering = lax.all_to_all(jnp.stack(entering), "seq", 0, 0, tiled=True)
    whole = [
        jnp.transpose(v, (1, 0, 2, 3)).reshape(heads_dev, HEAD_DIM, STATE)
        for v in (entering, second)
    ]
    return whole[0], whole[1], code


def mix_kernel(
    place,
    size,
    seq_ref,
    code_ref,
    total_ref,
    x_ref,
    z_ref,
    b_ref,
    c_ref,
    run_ref,
    run_t_ref,
    step_t_ref,
    gain_ref,
    own_ref,
    *refs,
):
    entered, second = refs[:size], refs[size : 2 * size]
    out_ref, state, mixed = refs[2 * size :]
    block = pl.program_id(1)
    width = x_ref.shape[1]
    heads = run_ref.shape[2]
    head = (place + pl.program_id(0)) * heads

    def put(pieces):
        part = pieces[0].shape[1]
        for d in range(size):
            source = seq_ref[0] - d
            source = jnp.where(source < 0, source + size, source)
            start = pl.multiple_of(source * part, part)
            for h in range(heads):
                state[pl.ds(h * HEAD_DIM + start, part), :] = pieces[d][h].astype(F32)

    @pl.when(block == 0)
    def _():
        put(entered)

    @pl.when(block > 0)
    def _():
        @pl.when(code_ref[0] == 1)
        def _():
            put(second)

        @pl.when(code_ref[0] == 0)
        def _():
            for h in range(heads):
                rows = pl.ds(h * HEAD_DIM, HEAD_DIM)
                state[rows, :] = total_ref[0, head + h] * state[rows, :] + own_ref[0, rows, :]

    read = c_ref[...]
    scores = lax.dot_general(
        read, b_ref[...], (((1,), (1,)), ((), ())), preferred_element_type=F32
    )
    running = run_ref[0]
    inflow = lax.dot_general(
        read, state[...].astype(BF), (((1,), (1,)), ((), ())), preferred_element_type=F32
    )
    mixed[...] = inflow * widen(jnp.exp(running), width)
    row = lax.broadcasted_iota(jnp.int32, (STRETCH, STRETCH), 0)
    col = lax.broadcasted_iota(jnp.int32, (STRETCH, STRETCH), 1)
    lower = row >= col
    lane = lax.broadcasted_iota(jnp.int32, (STRETCH, 2 * HEAD_DIM), 1)
    for pair in range(heads // 2):
        mixes = []
        for h in (2 * pair, 2 * pair + 1):
            spread = running[:, h : h + 1] - run_t_ref[0, h : h + 1, :]
            fading = jnp.exp(jnp.where(lower, spread, -1e30))
            mixes.append((scores * fading * step_t_ref[0, h : h + 1, :]).astype(BF))
        lanes = pl.ds(pair * 2 * HEAD_DIM, 2 * HEAD_DIM)
        two = x_ref[:, lanes]
        none = jnp.zeros_like(two)
        stacked = jnp.concatenate(
            [jnp.where(lane < HEAD_DIM, two, none), jnp.where(lane < HEAD_DIM, none, two)], axis=0
        )
        mixed[:, lanes] += jnp.dot(
            jnp.concatenate(mixes, axis=1), stacked, preferred_element_type=F32
        )
    gate = z_ref[...].astype(F32)
    gated = mixed[...] * (gate / (1.0 + jnp.exp(-gate)))
    scale = lax.rsqrt(jnp.mean(gated * gated, axis=1, keepdims=True) + 1e-05)
    out_ref[...] = (gated * scale * gain_ref[...]).astype(BF)


def mix_groups(place, seq, code, totals, x, z, b, c, run, run_t, step_t, gain, own, entered, second):
    tokens, width = x.shape
    groups_dev = b.shape[1] // STATE
    per = width // groups_dev
    heads = run.shape[2]
    size = len(entered)
    smem = pl.BlockSpec(memory_space=pltpu.SMEM)
    piece = pl.BlockSpec((heads,) + entered[0].shape[1:], lambda g, i: (place + g, 0, 0))
    wide = pl.BlockSpec((STRETCH, per), lambda g, i: (i, place + g))
    basis = pl.BlockSpec((STRETCH, STATE), lambda g, i: (i, place + g))
    rows = pl.BlockSpec((1, heads, STRETCH), lambda g, i: (place + g, 0, i))
    return pl.pallas_call(
        functools.partial(mix_kernel, place, size),
        grid=(1, tokens // STRETCH),
        in_specs=[
            smem,
            smem,
            smem,
            wide,
            wide,
            basis,
            basis,
            pl.BlockSpec((1, STRETCH, heads), lambda g, i: (place + g, i, 0)),
            rows,
            rows,
            pl.BlockSpec((1, per), lambda g, i: (0, place + g)),
            pl.BlockSpec((1, per, STATE), lambda g, i: (0, place + g, 0)),
        ]
        + [piece] * (2 * size),
        out_specs=pl.BlockSpec((STRETCH, per), lambda g, i: (i, g)),
        out_shape=jax.ShapeDtypeStruct((tokens, per), BF),
        scratch_shapes=[pltpu.VMEM((per, STATE), F32), pltpu.VMEM((STRETCH, per), F32)],
        compiler_params=pltpu.CompilerParams(vmem_limit_bytes=VMEM_LIMIT),
        cost_estimate=SMALL,
    )(seq.reshape(1), code, totals, x, z, b, c, run, run_t, step_t, gain, own, *entered, *second)


def project_kernel(first_ref, *refs):
    weights, near_ref, far_ref, rows_all, weight, total, sems = refs[-7:]
    lhs = refs[:-7]
    tokens, depth = lhs[0].shape
    cols = weights.shape[2]
    parts = len(lhs) // 4
    for part in range(parts):
        span = pl.ds(part * depth, depth)
        for r in range(4):
            pltpu.make_async_copy(
                lhs[4 * part + r],
                rows_all.at[part, pl.ds(r * tokens, tokens)],
                sems.at[0, part],
            ).start()
        for n in range(2):
            pltpu.make_async_copy(
                weights.at[first_ref[0] + n, span],
                weight.at[part, :, pl.ds(n * cols, cols)],
                sems.at[1, part],
            ).start()
    for part in range(parts):
        pltpu.make_async_copy(rows_all.at[part], rows_all.at[part], sems.at[0, part]).wait()
        pltpu.make_async_copy(weight.at[part], weight.at[part], sems.at[1, part]).wait()
        for r in range(4):
            span = pl.ds(r * tokens, tokens)
            product = jnp.dot(rows_all[part, span, :], weight[part], preferred_element_type=F32)
            if part == 0:
                total[span, :] = product
            elif part < parts - 1:
                total[span, :] += product
            else:
                out_ref = far_ref if r >= 2 else near_ref
                out_ref[pl.ds(r % 2 * tokens, tokens), :] = (total[span, :] + product).astype(BF)


def project(first, lhs, weights):
    parts = len(lhs) // 4
    tokens = 4 * lhs[0].shape[0]
    depth, cols = weights.shape[1:]
    hbm = pl.BlockSpec(memory_space=pl.ANY)
    return pl.pallas_call(
        project_kernel,
        in_specs=[pl.BlockSpec(memory_space=pltpu.SMEM)] + [hbm] * (len(lhs) + 1),
        out_specs=[pl.BlockSpec(memory_space=pltpu.VMEM)] * 2,
        out_shape=[jax.ShapeDtypeStruct((tokens // 2, 2 * cols), BF)] * 2,
        scratch_shapes=[
            pltpu.VMEM((parts, tokens, depth // parts), BF),
            pltpu.VMEM((parts, depth // parts, 2 * cols), BF),
            pltpu.VMEM((tokens, 2 * cols), F32),
            pltpu.SemaphoreType.DMA((2, parts)),
        ],
        compiler_params=pltpu.CompilerParams(vmem_limit_bytes=VMEM_LIMIT),
        cost_estimate=SMALL,
    )(first.reshape(1), *lhs, weights)


SWAP = [(0, 1), (1, 0)]


def after(value, *others):
    return lax.optimization_barrier((value, *others))[0]


def to_rows(own, others, tokens):
    far, near = [
        (own[k].astype(F32) + lax.ppermute(others[k], "head", SWAP).astype(F32)).astype(BF)
        for k in (1, 0)
    ]
    from_y = lax.ppermute(far, "groups", SWAP).reshape(2, tokens, -1)
    near = near.reshape(2, tokens, -1)
    from_core = lax.ppermute(jnp.stack([near[1], from_y[1]]), "batch", SWAP)
    return near[0], from_core[0], from_y[0], from_core[1]


def in_order(y, core, parts):
    a, b, c, d = parts
    p = [jnp.where(core == 0, a, b), jnp.where(core == 0, b, a)]
    q = [jnp.where(core == 0, c, d), jnp.where(core == 0, d, c)]
    return [jnp.where(y == 0, v, w) for v, w in zip(p + q, q + p)]


def plain_projection(normed, out_weight):
    tokens = normed.shape[0]
    pairs = lax.axis_size("batch")
    batch_index = lax.axis_index("batch")
    part_cols = out_weight.shape[1] // pairs
    own_part = lax.dynamic_slice_in_dim(out_weight, batch_index * part_cols, part_cols, 1)
    both_rows = lax.all_gather(normed, "batch", axis=0, tiled=True)
    partial_value = jnp.dot(
        both_rows,
        lax.all_gather(own_part, "seq", axis=1, tiled=True),
        preferred_element_type=F32,
    )
    summed = lax.psum_scatter(partial_value.astype(BF), "head", scatter_dimension=1, tiled=True)
    spans = summed.shape[1] // part_cols
    sections = summed.reshape(pairs, tokens, spans, 1, part_cols)
    regrouped = lax.all_to_all(sections, "batch", split_axis=0, concat_axis=3, tiled=True)
    return regrouped.reshape(1, tokens, spans * pairs * part_cols)


def exchange_states(payload, seq, size):
    return [
        lax.ppermute(piece, "seq", [(i, (i + offset) % size) for i in range(size)])
        if offset
        else piece
        for offset, piece in enumerate(payload)
    ]


def body(
    x_values,
    z_gate,
    write_basis,
    read_basis,
    step_size,
    log_decay,
    cached_states,
    session_slots,
    conv_lengths,
    norm_gain,
    out_weight,
):
    tokens = x_values.shape[1]
    width = x_values.shape[2]
    heads_dev = step_size.shape[2]
    groups_dev = write_basis.shape[2] // STATE
    per_group = heads_dev // groups_dev
    per = width // groups_dev
    blocks = tokens // STRETCH
    size = lax.axis_size("seq")
    seq = lax.axis_index("seq")
    assert blocks == 2

    shared = lax.axis_size("groups") * lax.axis_size("batch")
    fast = (
        size == 4
        and lax.axis_size("head") == 2
        and shared == 4
        and out_weight.shape == (4096, 1024)
        and groups_dev == 4
    )
    kernels = HEAD_DIM // size % 16 == 0 and 2 * heads_dev <= STATE
    if kernels:
        second, code = second_states(seq, conv_lengths, session_slots, cached_states, size)
        second = exchange_states(second, seq, size)
    head = lax.axis_index("head")
    y = lax.axis_index("groups")
    core = lax.axis_index("batch")

    logs = log_decay[0].reshape(blocks, STRETCH, heads_dev)
    running = jnp.cumsum(logs, axis=1)
    totals = jnp.exp(running[:, -1, :])
    to_end = (jnp.exp(running[:, -1:, :] - running)).reshape(tokens, heads_dev) * step_size[0]
    run = running.reshape(tokens, groups_dev, per_group)
    by_group = jnp.transpose(run, (1, 0, 2))
    by_row = jnp.transpose(run, (1, 2, 0))
    step_t = jnp.transpose(step_size[0].reshape(tokens, groups_dev, per_group), (1, 2, 0))
    end_g = jnp.transpose(to_end.reshape(tokens, groups_dev, per_group), (1, 0, 2))

    x, z, b, c = x_values[0], z_gate[0], write_basis[0], read_basis[0]
    own = block_states_of(x, b, end_g, blocks)
    if fast:
        quarter = out_weight.shape[1] // 4
        piece = quarter // PIECES
        w_own = [
            lax.dynamic_slice_in_dim(
                out_weight, (2 * y + core) * quarter + k * piece, piece, 1
            )
            for k in range(PIECES)
        ]

    if kernels:
        both = jnp.concatenate([totals[0] * totals[1], totals[1]])
        both = jnp.pad(both, (0, STATE - 2 * heads_dev))
        high = both.astype(BF)
        low = (both - high.astype(F32)).astype(BF)
        gains = jnp.pad(jnp.stack([high, low]), ((0, HEAD_DIM // size - 2), (0, 0)))
        added = split_states(seq, code, totals, gains, own, per, size)
        added = exchange_states([after(v, *second) for v in added], seq, size)
        entered = entering_states(seq, conv_lengths, session_slots, cached_states, added)
        entered = exchange_states(entered, seq, size)
    else:
        one, two, code = plain_entering(
            seq, conv_lengths, session_slots, cached_states, totals, own, size
        )
        entered, second = [one], [two]
    where = seq if kernels else jnp.zeros_like(seq)
    if fast:
        weights = [lax.all_gather(part, "seq", axis=0) for part in w_own]
    gain = norm_gain.reshape(1, width)
    normed = [
        mix_groups(
            g, where, code, totals, x, z, b, c, by_group, by_row, step_t, gain, own, entered, second
        )
        for g in range(groups_dev)
    ]
    if not fast:
        return plain_projection(jnp.concatenate(normed, axis=1), out_weight)

    lhs = []
    for part in normed:
        across = lax.ppermute(part, "groups", SWAP)
        other = lax.ppermute(part, "batch", SWAP)
        other_across = lax.ppermute(across, "batch", SWAP)
        lhs += [part, other, across, other_across]
    sides = []
    done = []
    for part in weights:
        others = project(2 - 2 * head, lhs, after(part, *done))
        mine = project(2 * head, lhs, after(part, *others) if done else part)
        done = mine
        sides.append(in_order(y, core, to_rows(mine, others, tokens)))
    pieces = [
        sides[k][q][:, block * piece : (block + 1) * piece]
        for block in range(2)
        for q in range(4)
        for k in range(PIECES)
    ]
    return jnp.concatenate(pieces, axis=1)[None]


def solution(mesh):
    placed = (
        P(("groups", "batch"), "seq", "head"),
        P(("groups", "batch"), "seq", "head"),
        P(("groups", "batch"), "seq", "head"),
        P(("groups", "batch"), "seq", "head"),
        P(("groups", "batch"), "seq", "head"),
        P(("groups", "batch"), "seq", "head"),
        P(("groups", "batch"), None, "head", "seq", None),
        P(("groups", "batch"), None),
        P(("groups", "batch"), None),
        P("head"),
        P("head", "seq"),
    )
    return jax.shard_map(
        body,
        mesh=mesh,
        in_specs=placed,
        out_specs=P(("groups", "batch"), "seq", "head"),
        check_vma=False,
    )
```

```python
import functools

import jax
import jax.numpy as jnp
from jax import lax
from jax.experimental import pallas as pl
from jax.experimental.pallas import tpu as pltpu
from jax.sharding import PartitionSpec as P

HEAD_DIM = 64
STATE = 128
STRETCH = 128
PIECES = 2
BF = jnp.bfloat16
F32 = jnp.float32
VMEM_LIMIT = 56 * 1024 * 1024
SMALL = pl.CostEstimate(flops=1000, bytes_accessed=1000, transcendentals=0)


def widen(per_head, width):
    heads = per_head.shape[1]
    high = per_head.astype(BF)
    low = (per_head - high.astype(F32)).astype(BF)
    both = jnp.concatenate([high, low], axis=1)
    place = lax.broadcasted_iota(jnp.int32, (2 * heads, width), 0)
    lane = lax.broadcasted_iota(jnp.int32, (2 * heads, width), 1)
    place = jnp.where(place >= heads, place - heads, place)
    spread = jnp.where(place == lane // (width // heads), 1.0, 0.0).astype(BF)
    return jnp.dot(both, spread, preferred_element_type=F32)


def states_kernel(x_ref, b_ref, end_ref, out_ref):
    width = x_ref.shape[1]
    for c in range(out_ref.shape[0]):
        rows = pl.ds(c * STRETCH, STRETCH)
        scaled = (x_ref[rows, :].astype(F32) * widen(end_ref[0, rows, :], width)).astype(BF)
        out_ref[c] = lax.dot_general(
            scaled, b_ref[rows, :], (((0,), (0,)), ((), ())), preferred_element_type=F32
        )


def block_states_of(x, b, to_end, blocks):
    tokens, width = x.shape
    groups_dev = b.shape[1] // STATE
    per = width // groups_dev
    return pl.pallas_call(
        states_kernel,
        grid=(groups_dev,),
        in_specs=[
            pl.BlockSpec((tokens, per), lambda g: (0, g)),
            pl.BlockSpec((tokens, STATE), lambda g: (0, g)),
            pl.BlockSpec((1, tokens, to_end.shape[2]), lambda g: (g, 0, 0)),
        ],
        out_specs=pl.BlockSpec((blocks, per, STATE), lambda g: (0, g, 0)),
        out_shape=jax.ShapeDtypeStruct((blocks, width, STATE), F32),
        compiler_params=pltpu.CompilerParams(vmem_limit_bytes=VMEM_LIMIT),
        cost_estimate=pl.CostEstimate(
            flops=2 * tokens * width * STATE, bytes_accessed=16 << 20, transcendentals=0
        ),
    )(x, b, to_end)


def row_starts(lengths_ref, slots_ref):
    convs = lengths_ref.shape[1]
    begins = [jnp.int32(0)]
    for j in range(convs - 1):
        begins.append(begins[-1] + lengths_ref[0, j])

    def starts(block):
        found = begins[0] == block
        for begin in begins[1:]:
            found = jnp.logical_or(found, begin == block)
        return found

    def slot(block):
        entry = slots_ref[0, 0]
        for j in range(1, convs):
            entry = jnp.where(begins[j] <= block, slots_ref[0, j], entry)
        return entry

    return starts, slot


def along(seq, offset, size):
    place = seq + offset
    return jnp.where(place >= size, place - size, place)


def second_kernel(size, seq_ref, lengths_ref, slots_ref, cached, *refs):
    pieces, code_ref, sems = refs[:size], refs[size], refs[-1]
    starts, slot = row_starts(lengths_ref, slots_ref)
    seq = seq_ref[0]
    copies = []
    for offset in range(size):
        entry = slot(2 * along(seq, offset, size) + 1)
        copies.append(pltpu.make_async_copy(cached.at[0, entry], pieces[offset], sems.at[offset]))
        copies[-1].start()
    code_ref[0] = jnp.where(starts(2 * seq + 1), 1, 0).astype(jnp.int32)
    for copy in copies:
        copy.wait()


def second_states(seq, lengths, slots, cached, size):
    smem = pl.BlockSpec(memory_space=pltpu.SMEM)
    whole = pl.BlockSpec(memory_space=pltpu.VMEM)
    piece = jax.ShapeDtypeStruct(cached.shape[2:], cached.dtype)
    *pieces, code = pl.pallas_call(
        functools.partial(second_kernel, size),
        in_specs=[smem, smem, smem, pl.BlockSpec(memory_space=pl.ANY)],
        out_specs=[whole] * size + [smem],
        out_shape=[piece] * size + [jax.ShapeDtypeStruct((1,), jnp.int32)],
        scratch_shapes=[pltpu.SemaphoreType.DMA((size,))],
        cost_estimate=SMALL,
    )(seq.reshape(1), lengths, slots, cached)
    return pieces, code


def split_kernel(size, seq_ref, code_ref, total_ref, gain_ref, own_ref, *refs):
    pieces, added = refs[:size], refs[size]
    group = pl.program_id(0)
    per = own_ref.shape[1]
    heads = per // HEAD_DIM
    part = HEAD_DIM // size
    for h in range(heads):
        rows = pl.ds(h * HEAD_DIM, HEAD_DIM)
        gain = jnp.where(code_ref[0] == 1, 0.0, total_ref[1, group * heads + h])
        added[rows, :] = (own_ref[0, rows, :] * gain + own_ref[1, rows, :]).astype(BF)
    for d in range(size):
        start = along(seq_ref[0], d, size) * part
        for h in range(heads):
            rows = pl.ds(pl.multiple_of(h * HEAD_DIM + start, part), part)
            pieces[d][group * heads + h] = added[rows, :]

    @pl.when(group == 0)
    def _():
        for piece in pieces:
            piece[piece.shape[0] - 1] = gain_ref[...]


def split_states(seq, code, totals, gains, own, per, size):
    width = own.shape[1]
    heads_dev = width // HEAD_DIM
    smem = pl.BlockSpec(memory_space=pltpu.SMEM)
    whole = pl.BlockSpec(memory_space=pltpu.VMEM)
    shape = (heads_dev + 1, HEAD_DIM // size, STATE)
    return pl.pallas_call(
        functools.partial(split_kernel, size),
        grid=(width // per,),
        in_specs=[smem, smem, smem, whole, pl.BlockSpec((2, per, STATE), lambda g: (0, g, 0))],
        out_specs=[pl.BlockSpec(shape, lambda g: (0, 0, 0))] * size,
        out_shape=[jax.ShapeDtypeStruct(shape, BF)] * size,
        scratch_shapes=[pltpu.VMEM((per, STATE), BF)],
        compiler_params=pltpu.CompilerParams(vmem_limit_bytes=VMEM_LIMIT),
        cost_estimate=SMALL,
    )(seq.reshape(1), code, totals, gains, own)


def enter_kernel(size, seq_ref, lengths_ref, slots_ref, cached_ref, *refs):
    pieces, outs, added, entering = refs[:size], refs[size : 2 * size], refs[-2], refs[-1]
    starts, slot = row_starts(lengths_ref, slots_ref)
    seq = seq_ref[0]
    heads_dev = cached_ref.shape[2]
    for d in range(size):
        source = seq - d
        added[jnp.where(source < 0, source + size, source)] = pieces[d][...]
    for t in range(size):
        if t:
            second = starts(2 * t - 1)
            before = slot(2 * t - 1)
            first = starts(2 * t)

            @pl.when(first)
            def _(t=t):
                entering[t] = cached_ref[0, slot(2 * t)]

            @pl.when(jnp.logical_not(first))
            def _(t=t, second=second, before=before):
                high = added[t - 1, heads_dev].astype(F32)
                gains = high[0:1, :] + high[1:2, :]
                for h in range(heads_dev):
                    both = gains[:, h : h + 1]
                    last = gains[:, heads_dev + h : heads_dev + h + 1]
                    old = jnp.where(
                        second,
                        cached_ref[0, before, h].astype(F32) * last,
                        entering[t - 1, h].astype(F32) * both,
                    )
                    entering[t, h] = (old + added[t - 1, h].astype(F32)).astype(BF)

        else:
            entering[0] = cached_ref[0, slot(0)]
    for d in range(size):
        outs[d][...] = entering[along(seq, d, size)]


def entering_states(seq, lengths, slots, cached, pieces):
    size = len(pieces)
    shape = cached.shape[2:]
    smem = pl.BlockSpec(memory_space=pltpu.SMEM)
    whole = pl.BlockSpec(memory_space=pltpu.VMEM)
    return pl.pallas_call(
        functools.partial(enter_kernel, size),
        in_specs=[smem, smem, smem] + [whole] * (size + 1),
        out_specs=[whole] * size,
        out_shape=[jax.ShapeDtypeStruct(shape, BF)] * size,
        scratch_shapes=[
            pltpu.VMEM((size,) + pieces[0].shape, BF),
            pltpu.VMEM((size,) + shape, BF),
        ],
        compiler_params=pltpu.CompilerParams(vmem_limit_bytes=VMEM_LIMIT),
        cost_estimate=SMALL,
    )(seq.reshape(1), lengths, slots, cached, *pieces)


def plain_entering(seq, lengths, slots, cached, totals, own, size):
    heads_dev, part = cached.shape[2:4]
    begins = jnp.cumsum(lengths[0]) - lengths[0]
    blocks = jnp.arange(2 * size, dtype=jnp.int32)
    starts = jnp.any(begins[None, :] == blocks[:, None], axis=1)
    owners = jnp.sum((begins[None, :] <= blocks[:, None]).astype(jnp.int32), axis=1) - 1
    entries = jnp.take(cached[0], jnp.take(slots[0], owners), axis=0)
    second = lax.all_to_all(entries[1::2], "seq", 0, 0, tiled=True)
    code = lax.dynamic_index_in_dim(starts, 2 * seq + 1, 0, True).astype(jnp.int32)
    states = own.reshape(2, heads_dev, HEAD_DIM, STATE)
    keep = jnp.where(code[0] == 1, 0.0, totals[1])[:, None, None]
    added = (keep * states[0] + states[1]).astype(BF)
    added = jnp.transpose(added.reshape(heads_dev, size, part, STATE), (1, 0, 2, 3))
    added = lax.all_to_all(added, "seq", 0, 0, tiled=True)
    gains = lax.all_gather(totals, "seq")
    entering = [entries[0]]
    for t in range(1, size):
        last = gains[t - 1, 1][:, None, None]
        both = (gains[t - 1, 0] * gains[t - 1, 1])[:, None, None]
        old = jnp.where(
            starts[2 * t - 1],
            entries[2 * t - 1].astype(F32) * last,
            entering[-1].astype(F32) * both,
        )
        carry = (old + added[t - 1].astype(F32)).astype(BF)
        entering.append(jnp.where(starts[2 * t], entries[2 * t], carry))
    entering = lax.all_to_all(jnp.stack(entering), "seq", 0, 0, tiled=True)
    whole = [
        jnp.transpose(v, (1, 0, 2, 3)).reshape(heads_dev, HEAD_DIM, STATE)
        for v in (entering, second)
    ]
    return whole[0], whole[1], code


def mix_kernel(
    place,
    size,
    seq_ref,
    code_ref,
    total_ref,
    x_ref,
    z_ref,
    b_ref,
    c_ref,
    run_ref,
    run_t_ref,
    step_t_ref,
    gain_ref,
    own_ref,
    *refs,
):
    entered, second = refs[:size], refs[size : 2 * size]
    out_ref, state, mixed = refs[2 * size :]
    block = pl.program_id(1)
    width = x_ref.shape[1]
    heads = run_ref.shape[2]
    head = (place + pl.program_id(0)) * heads

    def put(pieces):
        part = pieces[0].shape[1]
        for d in range(size):
            source = seq_ref[0] - d
            source = jnp.where(source < 0, source + size, source)
            start = pl.multiple_of(source * part, part)
            for h in range(heads):
                state[pl.ds(h * HEAD_DIM + start, part), :] = pieces[d][h].astype(F32)

    @pl.when(block == 0)
    def _():
        put(entered)

    @pl.when(block > 0)
    def _():
        @pl.when(code_ref[0] == 1)
        def _():
            put(second)

        @pl.when(code_ref[0] == 0)
        def _():
            for h in range(heads):
                rows = pl.ds(h * HEAD_DIM, HEAD_DIM)
                state[rows, :] = total_ref[0, head + h] * state[rows, :] + own_ref[0, rows, :]

    read = c_ref[...]
    scores = lax.dot_general(
        read, b_ref[...], (((1,), (1,)), ((), ())), preferred_element_type=F32
    )
    running = run_ref[0]
    inflow = lax.dot_general(
        read, state[...].astype(BF), (((1,), (1,)), ((), ())), preferred_element_type=F32
    )
    mixed[...] = inflow * widen(jnp.exp(running), width)
    row = lax.broadcasted_iota(jnp.int32, (STRETCH, STRETCH), 0)
    col = lax.broadcasted_iota(jnp.int32, (STRETCH, STRETCH), 1)
    lower = row >= col
    lane = lax.broadcasted_iota(jnp.int32, (STRETCH, 2 * HEAD_DIM), 1)
    for pair in range(heads // 2):
        mixes = []
        for h in (2 * pair, 2 * pair + 1):
            spread = running[:, h : h + 1] - run_t_ref[0, h : h + 1, :]
            fading = jnp.exp(jnp.where(lower, spread, -1e30))
            mixes.append((scores * fading * step_t_ref[0, h : h + 1, :]).astype(BF))
        lanes = pl.ds(pair * 2 * HEAD_DIM, 2 * HEAD_DIM)
        two = x_ref[:, lanes]
        none = jnp.zeros_like(two)
        stacked = jnp.concatenate(
            [jnp.where(lane < HEAD_DIM, two, none), jnp.where(lane < HEAD_DIM, none, two)], axis=0
        )
        mixed[:, lanes] += jnp.dot(
            jnp.concatenate(mixes, axis=1), stacked, preferred_element_type=F32
        )
    gate = z_ref[...].astype(F32)
    gated = mixed[...] * (gate / (1.0 + jnp.exp(-gate)))
    scale = lax.rsqrt(jnp.mean(gated * gated, axis=1, keepdims=True) + 1e-05)
    out_ref[...] = (gated * scale * gain_ref[...]).astype(BF)


def mix_groups(place, seq, code, totals, x, z, b, c, run, run_t, step_t, gain, own, entered, second):
    tokens, width = x.shape
    groups_dev = b.shape[1] // STATE
    per = width // groups_dev
    heads = run.shape[2]
    size = len(entered)
    smem = pl.BlockSpec(memory_space=pltpu.SMEM)
    piece = pl.BlockSpec((heads,) + entered[0].shape[1:], lambda g, i: (place + g, 0, 0))
    wide = pl.BlockSpec((STRETCH, per), lambda g, i: (i, place + g))
    basis = pl.BlockSpec((STRETCH, STATE), lambda g, i: (i, place + g))
    rows = pl.BlockSpec((1, heads, STRETCH), lambda g, i: (place + g, 0, i))
    return pl.pallas_call(
        functools.partial(mix_kernel, place, size),
        grid=(1, tokens // STRETCH),
        in_specs=[
            smem,
            smem,
            smem,
            wide,
            wide,
            basis,
            basis,
            pl.BlockSpec((1, STRETCH, heads), lambda g, i: (place + g, i, 0)),
            rows,
            rows,
            pl.BlockSpec((1, per), lambda g, i: (0, place + g)),
            pl.BlockSpec((1, per, STATE), lambda g, i: (0, place + g, 0)),
        ]
        + [piece] * (2 * size),
        out_specs=pl.BlockSpec((STRETCH, per), lambda g, i: (i, g)),
        out_shape=jax.ShapeDtypeStruct((tokens, per), BF),
        scratch_shapes=[pltpu.VMEM((per, STATE), F32), pltpu.VMEM((STRETCH, per), F32)],
        compiler_params=pltpu.CompilerParams(vmem_limit_bytes=VMEM_LIMIT),
        cost_estimate=SMALL,
    )(seq.reshape(1), code, totals, x, z, b, c, run, run_t, step_t, gain, own, *entered, *second)


def project_kernel(outs, first_ref, *refs):
    rows_all, weight, total, sems = refs[-4:]
    out_refs = refs[-4 - outs : -4]
    weights = refs[-5 - outs]
    lhs = refs[: -5 - outs]
    tokens, depth = lhs[0].shape
    cols = weights.shape[2]
    parts = weight.shape[0]
    count = len(lhs) // parts
    for part in range(parts):
        span = pl.ds(part * depth, depth)
        for r in range(count):
            pltpu.make_async_copy(
                lhs[count * part + r],
                rows_all.at[part, pl.ds(r * tokens, tokens)],
                sems.at[0, part],
            ).start()
        for n in range(2):
            pltpu.make_async_copy(
                weights.at[first_ref[0] + n, span],
                weight.at[part, :, pl.ds(n * cols, cols)],
                sems.at[1, part],
            ).start()
    for part in range(parts):
        pltpu.make_async_copy(rows_all.at[part], rows_all.at[part], sems.at[0, part]).wait()
        pltpu.make_async_copy(weight.at[part], weight.at[part], sems.at[1, part]).wait()
        for r in range(count):
            span = pl.ds(r * tokens, tokens)
            product = jnp.dot(rows_all[part, span, :], weight[part], preferred_element_type=F32)
            if part == 0:
                total[span, :] = product
            elif part < parts - 1:
                total[span, :] += product
            else:
                each = count // outs
                place = pl.ds(r % each * tokens, tokens)
                out_refs[r // each][place, :] = (total[span, :] + product).astype(BF)


def project(first, lhs, weights, outs):
    parts = len(lhs)
    flat = [rows for part in lhs for rows in part]
    tokens = len(lhs[0]) * flat[0].shape[0]
    depth, cols = weights.shape[1:]
    hbm = pl.BlockSpec(memory_space=pl.ANY)
    return pl.pallas_call(
        functools.partial(project_kernel, outs),
        in_specs=[pl.BlockSpec(memory_space=pltpu.SMEM)] + [hbm] * (len(flat) + 1),
        out_specs=[pl.BlockSpec(memory_space=pltpu.VMEM)] * outs,
        out_shape=[jax.ShapeDtypeStruct((tokens // outs, 2 * cols), BF)] * outs,
        scratch_shapes=[
            pltpu.VMEM((parts, tokens, depth // parts), BF),
            pltpu.VMEM((parts, depth // parts, 2 * cols), BF),
            pltpu.VMEM((tokens, 2 * cols), F32),
            pltpu.SemaphoreType.DMA((2, parts)),
        ],
        compiler_params=pltpu.CompilerParams(vmem_limit_bytes=VMEM_LIMIT),
        cost_estimate=pl.CostEstimate(
            flops=4 * tokens * depth * cols,
            bytes_accessed=2 * depth * (tokens + 2 * cols),
            transcendentals=0,
        ),
    )(first.reshape(1), *flat, weights)


SWAP = [(0, 1), (1, 0)]


def after(value, *others):
    return lax.optimization_barrier((value, *others))[0]


def to_rows(own, others, tokens, near_first):
    far = lax.ppermute(others[1], "head", SWAP)
    near = lax.ppermute(others[0] if near_first else after(others[0], far), "head", SWAP)
    far = (own[1].astype(F32) + far.astype(F32)).astype(BF)
    near = (own[0].astype(F32) + near.astype(F32)).astype(BF)
    from_y = lax.ppermute(far, "groups", SWAP).reshape(2, tokens, -1)
    near = near.reshape(2, tokens, -1)
    from_core = lax.ppermute(jnp.stack([near[1], from_y[1]]), "batch", SWAP)
    return near[0], from_core[0], from_y[0], from_core[1]


def in_order(y, core, parts):
    a, b, c, d = parts
    p = [jnp.where(core == 0, a, b), jnp.where(core == 0, b, a)]
    q = [jnp.where(core == 0, c, d), jnp.where(core == 0, d, c)]
    return [jnp.where(y == 0, v, w) for v, w in zip(p + q, q + p)]


def plain_projection(normed, out_weight):
    tokens = normed.shape[0]
    pairs = lax.axis_size("batch")
    batch_index = lax.axis_index("batch")
    part_cols = out_weight.shape[1] // pairs
    own_part = lax.dynamic_slice_in_dim(out_weight, batch_index * part_cols, part_cols, 1)
    both_rows = lax.all_gather(normed, "batch", axis=0, tiled=True)
    partial_value = jnp.dot(
        both_rows,
        lax.all_gather(own_part, "seq", axis=1, tiled=True),
        preferred_element_type=F32,
    )
    summed = lax.psum_scatter(partial_value.astype(BF), "head", scatter_dimension=1, tiled=True)
    spans = summed.shape[1] // part_cols
    sections = summed.reshape(pairs, tokens, spans, 1, part_cols)
    regrouped = lax.all_to_all(sections, "batch", split_axis=0, concat_axis=3, tiled=True)
    return regrouped.reshape(1, tokens, spans * pairs * part_cols)


def exchange_states(payload, seq, size):
    return [
        lax.ppermute(piece, "seq", [(i, (i + offset) % size) for i in range(size)])
        if offset
        else piece
        for offset, piece in enumerate(payload)
    ]


def body(
    x_values,
    z_gate,
    write_basis,
    read_basis,
    step_size,
    log_decay,
    cached_states,
    session_slots,
    conv_lengths,
    norm_gain,
    out_weight,
):
    tokens = x_values.shape[1]
    width = x_values.shape[2]
    heads_dev = step_size.shape[2]
    groups_dev = write_basis.shape[2] // STATE
    per_group = heads_dev // groups_dev
    per = width // groups_dev
    blocks = tokens // STRETCH
    size = lax.axis_size("seq")
    seq = lax.axis_index("seq")
    assert blocks == 2

    shared = lax.axis_size("groups") * lax.axis_size("batch")
    fast = (
        size == 4
        and lax.axis_size("head") == 2
        and shared == 4
        and out_weight.shape == (4096, 1024)
        and groups_dev == 4
    )
    kernels = HEAD_DIM // size % 16 == 0 and 2 * heads_dev <= STATE
    if kernels:
        second, code = second_states(seq, conv_lengths, session_slots, cached_states, size)
        second = exchange_states(second, seq, size)
    head = lax.axis_index("head")
    y = lax.axis_index("groups")
    core = lax.axis_index("batch")

    logs = log_decay[0].reshape(blocks, STRETCH, heads_dev)
    running = jnp.cumsum(logs, axis=1)
    totals = jnp.exp(running[:, -1, :])
    to_end = (jnp.exp(running[:, -1:, :] - running)).reshape(tokens, heads_dev) * step_size[0]
    run = running.reshape(tokens, groups_dev, per_group)
    by_group = jnp.transpose(run, (1, 0, 2))
    by_row = jnp.transpose(run, (1, 2, 0))
    step_t = jnp.transpose(step_size[0].reshape(tokens, groups_dev, per_group), (1, 2, 0))
    end_g = jnp.transpose(to_end.reshape(tokens, groups_dev, per_group), (1, 0, 2))

    x, z, b, c = x_values[0], z_gate[0], write_basis[0], read_basis[0]
    own = block_states_of(x, b, end_g, blocks)
    if fast:
        quarter = out_weight.shape[1] // 4
        piece = quarter // PIECES
        w_own = [
            lax.dynamic_slice_in_dim(
                out_weight, (2 * y + core) * quarter + k * piece, piece, 1
            )
            for k in range(PIECES)
        ]

    if kernels:
        both = jnp.concatenate([totals[0] * totals[1], totals[1]])
        both = jnp.pad(both, (0, STATE - 2 * heads_dev))
        high = both.astype(BF)
        low = (both - high.astype(F32)).astype(BF)
        gains = jnp.pad(jnp.stack([high, low]), ((0, HEAD_DIM // size - 2), (0, 0)))
        added = split_states(seq, code, totals, gains, own, per, size)
        added = exchange_states([after(v, *second) for v in added], seq, size)
        entered = entering_states(seq, conv_lengths, session_slots, cached_states, added)
        entered = exchange_states(entered, seq, size)
    else:
        one, two, code = plain_entering(
            seq, conv_lengths, session_slots, cached_states, totals, own, size
        )
        entered, second = [one], [two]
    where = seq if kernels else jnp.zeros_like(seq)
    if fast:
        weights = [lax.all_gather(part, "seq", axis=0) for part in w_own]
    gain = norm_gain.reshape(1, width)
    normed = [
        mix_groups(
            g, where, code, totals, x, z, b, c, by_group, by_row, step_t, gain, own, entered, second
        )
        for g in range(groups_dev)
    ]
    if not fast:
        return plain_projection(jnp.concatenate(normed, axis=1), out_weight)

    theirs, mine = 2 - 2 * head, 2 * head
    crossed = [lax.ppermute(part, "groups", SWAP) for part in normed]
    near = []
    for n, part in enumerate(normed):
        tied = after(part, *crossed[max(n - 2, 0) : n - 1]) if n > 1 else part
        near.append([part, lax.ppermute(tied, "batch", SWAP)])
    near_others = project(theirs, near, weights[0], 1)
    near_mine = project(mine, near, weights[0], 1)
    far = []
    for across in crossed:
        across = after(across, *near_mine)
        far.append([across, lax.ppermute(across, "batch", SWAP)])
    far_others = project(theirs, far, weights[0], 1)
    lhs = [a + b for a, b in zip(near, far)]
    far_mine = project(mine, far, after(weights[0], *far_others), 1)
    last = after(weights[1], *far_mine)
    last_others = project(theirs, lhs, last, 2)
    last_mine = project(mine, lhs, after(last, *last_others), 2)
    sides = [
        in_order(y, core, to_rows(near_mine + far_mine, near_others + far_others, tokens, True)),
        in_order(y, core, to_rows(last_mine, last_others, tokens, False)),
    ]
    pieces = [
        sides[k][q][:, block * piece : (block + 1) * piece]
        for block in range(2)
        for q in range(4)
        for k in range(PIECES)
    ]
    return jnp.concatenate(pieces, axis=1)[None]


def solution(mesh):
    placed = (
        P(("groups", "batch"), "seq", "head"),
        P(("groups", "batch"), "seq", "head"),
        P(("groups", "batch"), "seq", "head"),
        P(("groups", "batch"), "seq", "head"),
        P(("groups", "batch"), "seq", "head"),
        P(("groups", "batch"), "seq", "head"),
        P(("groups", "batch"), None, "head", "seq", None),
        P(("groups", "batch"), None),
        P(("groups", "batch"), None),
        P("head"),
        P("head", "seq"),
    )
    return jax.shard_map(
        body,
        mesh=mesh,
        in_specs=placed,
        out_specs=P(("groups", "batch"), "seq", "head"),
        check_vma=False,
    )
```

```python
import functools

import jax
import jax.numpy as jnp
from jax import lax
from jax.experimental import pallas as pl
from jax.experimental.pallas import tpu as pltpu
from jax.sharding import PartitionSpec as P

HEAD_DIM = 64
STATE = 128
STRETCH = 128
PIECES = 2
BF = jnp.bfloat16
F32 = jnp.float32
VMEM_LIMIT = 56 * 1024 * 1024
SMALL = pl.CostEstimate(flops=1000, bytes_accessed=1000, transcendentals=0)


def widen(per_head, width):
    heads = per_head.shape[1]
    high = per_head.astype(BF)
    low = (per_head - high.astype(F32)).astype(BF)
    both = jnp.concatenate([high, low], axis=1)
    place = lax.broadcasted_iota(jnp.int32, (2 * heads, width), 0)
    lane = lax.broadcasted_iota(jnp.int32, (2 * heads, width), 1)
    place = jnp.where(place >= heads, place - heads, place)
    spread = jnp.where(place == lane // (width // heads), 1.0, 0.0).astype(BF)
    return jnp.dot(both, spread, preferred_element_type=F32)


def states_kernel(x_ref, b_ref, end_ref, out_ref):
    width = x_ref.shape[1]
    for c in range(out_ref.shape[0]):
        rows = pl.ds(c * STRETCH, STRETCH)
        scaled = (x_ref[rows, :].astype(F32) * widen(end_ref[0, rows, :], width)).astype(BF)
        out_ref[c] = lax.dot_general(
            scaled, b_ref[rows, :], (((0,), (0,)), ((), ())), preferred_element_type=F32
        )


def block_states_of(x, b, to_end, blocks):
    tokens, width = x.shape
    groups_dev = b.shape[1] // STATE
    per = width // groups_dev
    return pl.pallas_call(
        states_kernel,
        grid=(groups_dev,),
        in_specs=[
            pl.BlockSpec((tokens, per), lambda g: (0, g)),
            pl.BlockSpec((tokens, STATE), lambda g: (0, g)),
            pl.BlockSpec((1, tokens, to_end.shape[2]), lambda g: (g, 0, 0)),
        ],
        out_specs=pl.BlockSpec((blocks, per, STATE), lambda g: (0, g, 0)),
        out_shape=jax.ShapeDtypeStruct((blocks, width, STATE), F32),
        compiler_params=pltpu.CompilerParams(vmem_limit_bytes=VMEM_LIMIT),
        cost_estimate=pl.CostEstimate(
            flops=2 * tokens * width * STATE, bytes_accessed=16 << 20, transcendentals=0
        ),
    )(x, b, to_end)


def row_starts(lengths_ref, slots_ref):
    convs = lengths_ref.shape[1]
    begins = [jnp.int32(0)]
    for j in range(convs - 1):
        begins.append(begins[-1] + lengths_ref[0, j])

    def starts(block):
        found = begins[0] == block
        for begin in begins[1:]:
            found = jnp.logical_or(found, begin == block)
        return found

    def slot(block):
        entry = slots_ref[0, 0]
        for j in range(1, convs):
            entry = jnp.where(begins[j] <= block, slots_ref[0, j], entry)
        return entry

    return starts, slot


def along(seq, offset, size):
    place = seq + offset
    return jnp.where(place >= size, place - size, place)


def second_kernel(size, seq_ref, lengths_ref, slots_ref, cached, *refs):
    pieces, code_ref, sems = refs[:size], refs[size], refs[-1]
    starts, slot = row_starts(lengths_ref, slots_ref)
    seq = seq_ref[0]
    copies = []
    for offset in range(size):
        entry = slot(2 * along(seq, offset, size) + 1)
        copies.append(pltpu.make_async_copy(cached.at[0, entry], pieces[offset], sems.at[offset]))
        copies[-1].start()
    code_ref[0] = jnp.where(starts(2 * seq + 1), 1, 0).astype(jnp.int32)
    for copy in copies:
        copy.wait()


def second_states(seq, lengths, slots, cached, size):
    smem = pl.BlockSpec(memory_space=pltpu.SMEM)
    whole = pl.BlockSpec(memory_space=pltpu.VMEM)
    piece = jax.ShapeDtypeStruct(cached.shape[2:], cached.dtype)
    *pieces, code = pl.pallas_call(
        functools.partial(second_kernel, size),
        in_specs=[smem, smem, smem, pl.BlockSpec(memory_space=pl.ANY)],
        out_specs=[whole] * size + [smem],
        out_shape=[piece] * size + [jax.ShapeDtypeStruct((1,), jnp.int32)],
        scratch_shapes=[pltpu.SemaphoreType.DMA((size,))],
        cost_estimate=SMALL,
    )(seq.reshape(1), lengths, slots, cached)
    return pieces, code


def split_kernel(size, seq_ref, code_ref, total_ref, gain_ref, own_ref, *refs):
    pieces, added = refs[:size], refs[size]
    group = pl.program_id(0)
    per = own_ref.shape[1]
    heads = per // HEAD_DIM
    part = HEAD_DIM // size
    for h in range(heads):
        rows = pl.ds(h * HEAD_DIM, HEAD_DIM)
        gain = jnp.where(code_ref[0] == 1, 0.0, total_ref[1, group * heads + h])
        added[rows, :] = (own_ref[0, rows, :] * gain + own_ref[1, rows, :]).astype(BF)
    for d in range(size):
        start = along(seq_ref[0], d, size) * part
        for h in range(heads):
            rows = pl.ds(pl.multiple_of(h * HEAD_DIM + start, part), part)
            pieces[d][group * heads + h] = added[rows, :]

    @pl.when(group == 0)
    def _():
        for piece in pieces:
            piece[piece.shape[0] - 1] = gain_ref[...]


def split_states(seq, code, totals, gains, own, per, size):
    width = own.shape[1]
    heads_dev = width // HEAD_DIM
    smem = pl.BlockSpec(memory_space=pltpu.SMEM)
    whole = pl.BlockSpec(memory_space=pltpu.VMEM)
    shape = (heads_dev + 1, HEAD_DIM // size, STATE)
    return pl.pallas_call(
        functools.partial(split_kernel, size),
        grid=(width // per,),
        in_specs=[smem, smem, smem, whole, pl.BlockSpec((2, per, STATE), lambda g: (0, g, 0))],
        out_specs=[pl.BlockSpec(shape, lambda g: (0, 0, 0))] * size,
        out_shape=[jax.ShapeDtypeStruct(shape, BF)] * size,
        scratch_shapes=[pltpu.VMEM((per, STATE), BF)],
        compiler_params=pltpu.CompilerParams(vmem_limit_bytes=VMEM_LIMIT),
        cost_estimate=SMALL,
    )(seq.reshape(1), code, totals, gains, own)


def enter_kernel(size, seq_ref, lengths_ref, slots_ref, cached_ref, *refs):
    pieces, outs, added, entering = refs[:size], refs[size : 2 * size], refs[-2], refs[-1]
    starts, slot = row_starts(lengths_ref, slots_ref)
    seq = seq_ref[0]
    heads_dev = cached_ref.shape[2]
    for d in range(size):
        source = seq - d
        added[jnp.where(source < 0, source + size, source)] = pieces[d][...]
    for t in range(size):
        if t:
            second = starts(2 * t - 1)
            before = slot(2 * t - 1)
            first = starts(2 * t)

            @pl.when(first)
            def _(t=t):
                entering[t] = cached_ref[0, slot(2 * t)]

            @pl.when(jnp.logical_not(first))
            def _(t=t, second=second, before=before):
                high = added[t - 1, heads_dev].astype(F32)
                gains = high[0:1, :] + high[1:2, :]
                for h in range(heads_dev):
                    both = gains[:, h : h + 1]
                    last = gains[:, heads_dev + h : heads_dev + h + 1]
                    old = jnp.where(
                        second,
                        cached_ref[0, before, h].astype(F32) * last,
                        entering[t - 1, h].astype(F32) * both,
                    )
                    entering[t, h] = (old + added[t - 1, h].astype(F32)).astype(BF)

        else:
            entering[0] = cached_ref[0, slot(0)]
    for d in range(size):
        outs[d][...] = entering[along(seq, d, size)]


def entering_states(seq, lengths, slots, cached, pieces):
    size = len(pieces)
    shape = cached.shape[2:]
    smem = pl.BlockSpec(memory_space=pltpu.SMEM)
    whole = pl.BlockSpec(memory_space=pltpu.VMEM)
    return pl.pallas_call(
        functools.partial(enter_kernel, size),
        in_specs=[smem, smem, smem] + [whole] * (size + 1),
        out_specs=[whole] * size,
        out_shape=[jax.ShapeDtypeStruct(shape, BF)] * size,
        scratch_shapes=[
            pltpu.VMEM((size,) + pieces[0].shape, BF),
            pltpu.VMEM((size,) + shape, BF),
        ],
        compiler_params=pltpu.CompilerParams(vmem_limit_bytes=VMEM_LIMIT),
        cost_estimate=SMALL,
    )(seq.reshape(1), lengths, slots, cached, *pieces)


def plain_entering(seq, lengths, slots, cached, totals, own, size):
    heads_dev, part = cached.shape[2:4]
    begins = jnp.cumsum(lengths[0]) - lengths[0]
    blocks = jnp.arange(2 * size, dtype=jnp.int32)
    starts = jnp.any(begins[None, :] == blocks[:, None], axis=1)
    owners = jnp.sum((begins[None, :] <= blocks[:, None]).astype(jnp.int32), axis=1) - 1
    entries = jnp.take(cached[0], jnp.take(slots[0], owners), axis=0)
    second = lax.all_to_all(entries[1::2], "seq", 0, 0, tiled=True)
    code = lax.dynamic_index_in_dim(starts, 2 * seq + 1, 0, True).astype(jnp.int32)
    states = own.reshape(2, heads_dev, HEAD_DIM, STATE)
    keep = jnp.where(code[0] == 1, 0.0, totals[1])[:, None, None]
    added = (keep * states[0] + states[1]).astype(BF)
    added = jnp.transpose(added.reshape(heads_dev, size, part, STATE), (1, 0, 2, 3))
    added = lax.all_to_all(added, "seq", 0, 0, tiled=True)
    gains = lax.all_gather(totals, "seq")
    entering = [entries[0]]
    for t in range(1, size):
        last = gains[t - 1, 1][:, None, None]
        both = (gains[t - 1, 0] * gains[t - 1, 1])[:, None, None]
        old = jnp.where(
            starts[2 * t - 1],
            entries[2 * t - 1].astype(F32) * last,
            entering[-1].astype(F32) * both,
        )
        carry = (old + added[t - 1].astype(F32)).astype(BF)
        entering.append(jnp.where(starts[2 * t], entries[2 * t], carry))
    entering = lax.all_to_all(jnp.stack(entering), "seq", 0, 0, tiled=True)
    whole = [
        jnp.transpose(v, (1, 0, 2, 3)).reshape(heads_dev, HEAD_DIM, STATE)
        for v in (entering, second)
    ]
    return whole[0], whole[1], code


def mix_kernel(
    place,
    size,
    seq_ref,
    code_ref,
    total_ref,
    x_ref,
    z_ref,
    b_ref,
    c_ref,
    run_ref,
    run_t_ref,
    step_t_ref,
    gain_ref,
    own_ref,
    *refs,
):
    entered, second = refs[:size], refs[size : 2 * size]
    out_ref, state, mixed = refs[2 * size :]
    block = pl.program_id(1)
    width = x_ref.shape[1]
    heads = run_ref.shape[2]
    head = (place + pl.program_id(0)) * heads

    def put(pieces):
        part = pieces[0].shape[1]
        for d in range(size):
            source = seq_ref[0] - d
            source = jnp.where(source < 0, source + size, source)
            start = pl.multiple_of(source * part, part)
            for h in range(heads):
                state[pl.ds(h * HEAD_DIM + start, part), :] = pieces[d][h].astype(F32)

    @pl.when(block == 0)
    def _():
        put(entered)

    @pl.when(block > 0)
    def _():
        @pl.when(code_ref[0] == 1)
        def _():
            put(second)

        @pl.when(code_ref[0] == 0)
        def _():
            for h in range(heads):
                rows = pl.ds(h * HEAD_DIM, HEAD_DIM)
                state[rows, :] = total_ref[0, head + h] * state[rows, :] + own_ref[0, rows, :]

    read = c_ref[...]
    scores = lax.dot_general(
        read, b_ref[...], (((1,), (1,)), ((), ())), preferred_element_type=F32
    )
    running = run_ref[0]
    inflow = lax.dot_general(
        read, state[...].astype(BF), (((1,), (1,)), ((), ())), preferred_element_type=F32
    )
    mixed[...] = inflow * widen(jnp.exp(running), width)
    row = lax.broadcasted_iota(jnp.int32, (STRETCH, STRETCH), 0)
    col = lax.broadcasted_iota(jnp.int32, (STRETCH, STRETCH), 1)
    lower = row >= col
    lane = lax.broadcasted_iota(jnp.int32, (STRETCH, 2 * HEAD_DIM), 1)
    for pair in range(heads // 2):
        mixes = []
        for h in (2 * pair, 2 * pair + 1):
            spread = running[:, h : h + 1] - run_t_ref[0, h : h + 1, :]
            fading = jnp.exp(jnp.where(lower, spread, -1e30))
            mixes.append((scores * fading * step_t_ref[0, h : h + 1, :]).astype(BF))
        lanes = pl.ds(pair * 2 * HEAD_DIM, 2 * HEAD_DIM)
        two = x_ref[:, lanes]
        none = jnp.zeros_like(two)
        stacked = jnp.concatenate(
            [jnp.where(lane < HEAD_DIM, two, none), jnp.where(lane < HEAD_DIM, none, two)], axis=0
        )
        mixed[:, lanes] += jnp.dot(
            jnp.concatenate(mixes, axis=1), stacked, preferred_element_type=F32
        )
    gate = z_ref[...].astype(F32)
    gated = mixed[...] * (gate / (1.0 + jnp.exp(-gate)))
    scale = lax.rsqrt(jnp.mean(gated * gated, axis=1, keepdims=True) + 1e-05)
    out_ref[...] = (gated * scale * gain_ref[...]).astype(BF)


def mix_groups(place, seq, code, totals, x, z, b, c, run, run_t, step_t, gain, own, entered, second):
    tokens, width = x.shape
    groups_dev = b.shape[1] // STATE
    per = width // groups_dev
    heads = run.shape[2]
    size = len(entered)
    smem = pl.BlockSpec(memory_space=pltpu.SMEM)
    piece = pl.BlockSpec((heads,) + entered[0].shape[1:], lambda g, i: (place + g, 0, 0))
    wide = pl.BlockSpec((STRETCH, per), lambda g, i: (i, place + g))
    basis = pl.BlockSpec((STRETCH, STATE), lambda g, i: (i, place + g))
    rows = pl.BlockSpec((1, heads, STRETCH), lambda g, i: (place + g, 0, i))
    return pl.pallas_call(
        functools.partial(mix_kernel, place, size),
        grid=(1, tokens // STRETCH),
        in_specs=[
            smem,
            smem,
            smem,
            wide,
            wide,
            basis,
            basis,
            pl.BlockSpec((1, STRETCH, heads), lambda g, i: (place + g, i, 0)),
            rows,
            rows,
            pl.BlockSpec((1, per), lambda g, i: (0, place + g)),
            pl.BlockSpec((1, per, STATE), lambda g, i: (0, place + g, 0)),
        ]
        + [piece] * (2 * size),
        out_specs=pl.BlockSpec((STRETCH, per), lambda g, i: (i, g)),
        out_shape=jax.ShapeDtypeStruct((tokens, per), BF),
        scratch_shapes=[pltpu.VMEM((per, STATE), F32), pltpu.VMEM((STRETCH, per), F32)],
        compiler_params=pltpu.CompilerParams(vmem_limit_bytes=VMEM_LIMIT),
        cost_estimate=SMALL,
    )(seq.reshape(1), code, totals, x, z, b, c, run, run_t, step_t, gain, own, *entered, *second)


def project_kernel(outs, first_ref, *refs):
    rows_all, weight, total, sems = refs[-4:]
    out_refs = refs[-4 - outs : -4]
    weights = refs[-5 - outs]
    lhs = refs[: -5 - outs]
    tokens, depth = lhs[0].shape
    cols = weights.shape[2]
    parts = weight.shape[0]
    count = len(lhs) // parts
    for part in range(parts):
        span = pl.ds(part * depth, depth)
        for r in range(count):
            pltpu.make_async_copy(
                lhs[count * part + r],
                rows_all.at[part, pl.ds(r * tokens, tokens)],
                sems.at[0, part],
            ).start()
        for n in range(weight.shape[2] // cols):
            pltpu.make_async_copy(
                weights.at[first_ref[n // 2] + n % 2, span],
                weight.at[part, :, pl.ds(n * cols, cols)],
                sems.at[1, part],
            ).start()
    for part in range(parts):
        pltpu.make_async_copy(rows_all.at[part], rows_all.at[part], sems.at[0, part]).wait()
        pltpu.make_async_copy(weight.at[part], weight.at[part], sems.at[1, part]).wait()
        for r in range(count):
            span = pl.ds(r * tokens, tokens)
            product = jnp.dot(rows_all[part, span, :], weight[part], preferred_element_type=F32)
            if part == 0:
                total[span, :] = product
            elif part < parts - 1:
                total[span, :] += product
            else:
                product = (total[span, :] + product).astype(BF)
                wide = product.shape[1] // (2 * cols)
                each = count // (outs // wide)
                place = pl.ds(r % each * tokens, tokens)
                for n in range(wide):
                    out_refs[r // each + n][place, :] = product[:, 2 * n * cols : 2 * (n + 1) * cols]


def project(firsts, lhs, weights, outs):
    parts = len(lhs)
    flat = [rows for part in lhs for rows in part]
    tokens = len(lhs[0]) * flat[0].shape[0]
    depth, cols = weights.shape[1:]
    width = 2 * cols * len(firsts)
    rows = tokens if len(firsts) > 1 else tokens // outs
    hbm = pl.BlockSpec(memory_space=pl.ANY)
    return pl.pallas_call(
        functools.partial(project_kernel, outs),
        in_specs=[pl.BlockSpec(memory_space=pltpu.SMEM)] + [hbm] * (len(flat) + 1),
        out_specs=[pl.BlockSpec(memory_space=pltpu.VMEM)] * outs,
        out_shape=[jax.ShapeDtypeStruct((rows, 2 * cols), BF)] * outs,
        scratch_shapes=[
            pltpu.VMEM((parts, tokens, depth // parts), BF),
            pltpu.VMEM((parts, depth // parts, width), BF),
            pltpu.VMEM((tokens, width), F32),
            pltpu.SemaphoreType.DMA((2, parts)),
        ],
        compiler_params=pltpu.CompilerParams(vmem_limit_bytes=VMEM_LIMIT),
        cost_estimate=pl.CostEstimate(
            flops=2 * tokens * depth * width,
            bytes_accessed=2 * depth * (tokens + width),
            transcendentals=0,
        ),
    )(jnp.stack(firsts), *flat, weights)


SWAP = [(0, 1), (1, 0)]


def after(value, *others):
    return lax.optimization_barrier((value, *others))[0]


def to_rows(own, others, tokens, near_first):
    far = lax.ppermute(others[1], "head", SWAP)
    near = lax.ppermute(others[0] if near_first else after(others[0], far), "head", SWAP)
    far = (own[1].astype(F32) + far.astype(F32)).astype(BF)
    if near_first:
        near = after(near, own[1])
    near = (own[0].astype(F32) + near.astype(F32)).astype(BF)
    from_y = lax.ppermute(far, "groups", SWAP).reshape(2, tokens, -1)
    near = near.reshape(2, tokens, -1)
    from_core = lax.ppermute(jnp.stack([near[1], from_y[1]]), "batch", SWAP)
    return near[0], from_core[0], from_y[0], from_core[1]


def in_order(y, core, parts):
    a, b, c, d = parts
    p = [jnp.where(core == 0, a, b), jnp.where(core == 0, b, a)]
    q = [jnp.where(core == 0, c, d), jnp.where(core == 0, d, c)]
    return [jnp.where(y == 0, v, w) for v, w in zip(p + q, q + p)]


def plain_projection(normed, out_weight):
    tokens = normed.shape[0]
    pairs = lax.axis_size("batch")
    batch_index = lax.axis_index("batch")
    part_cols = out_weight.shape[1] // pairs
    own_part = lax.dynamic_slice_in_dim(out_weight, batch_index * part_cols, part_cols, 1)
    both_rows = lax.all_gather(normed, "batch", axis=0, tiled=True)
    partial_value = jnp.dot(
        both_rows,
        lax.all_gather(own_part, "seq", axis=1, tiled=True),
        preferred_element_type=F32,
    )
    summed = lax.psum_scatter(partial_value.astype(BF), "head", scatter_dimension=1, tiled=True)
    spans = summed.shape[1] // part_cols
    sections = summed.reshape(pairs, tokens, spans, 1, part_cols)
    regrouped = lax.all_to_all(sections, "batch", split_axis=0, concat_axis=3, tiled=True)
    return regrouped.reshape(1, tokens, spans * pairs * part_cols)


def exchange_states(payload, seq, size):
    return [
        lax.ppermute(piece, "seq", [(i, (i + offset) % size) for i in range(size)])
        if offset
        else piece
        for offset, piece in enumerate(payload)
    ]


def body(
    x_values,
    z_gate,
    write_basis,
    read_basis,
    step_size,
    log_decay,
    cached_states,
    session_slots,
    conv_lengths,
    norm_gain,
    out_weight,
):
    tokens = x_values.shape[1]
    width = x_values.shape[2]
    heads_dev = step_size.shape[2]
    groups_dev = write_basis.shape[2] // STATE
    per_group = heads_dev // groups_dev
    per = width // groups_dev
    blocks = tokens // STRETCH
    size = lax.axis_size("seq")
    seq = lax.axis_index("seq")
    assert blocks == 2

    shared = lax.axis_size("groups") * lax.axis_size("batch")
    fast = (
        size == 4
        and lax.axis_size("head") == 2
        and shared == 4
        and out_weight.shape == (4096, 1024)
        and groups_dev == 4
    )
    kernels = HEAD_DIM // size % 16 == 0 and 2 * heads_dev <= STATE
    if kernels:
        second, code = second_states(seq, conv_lengths, session_slots, cached_states, size)
        second = exchange_states(second, seq, size)
    head = lax.axis_index("head")
    y = lax.axis_index("groups")
    core = lax.axis_index("batch")

    logs = log_decay[0].reshape(blocks, STRETCH, heads_dev)
    running = jnp.cumsum(logs, axis=1)
    totals = jnp.exp(running[:, -1, :])
    to_end = (jnp.exp(running[:, -1:, :] - running)).reshape(tokens, heads_dev) * step_size[0]
    run = running.reshape(tokens, groups_dev, per_group)
    by_group = jnp.transpose(run, (1, 0, 2))
    by_row = jnp.transpose(run, (1, 2, 0))
    step_t = jnp.transpose(step_size[0].reshape(tokens, groups_dev, per_group), (1, 2, 0))
    end_g = jnp.transpose(to_end.reshape(tokens, groups_dev, per_group), (1, 0, 2))

    x, z, b, c = x_values[0], z_gate[0], write_basis[0], read_basis[0]
    own = block_states_of(x, b, end_g, blocks)
    if fast:
        quarter = out_weight.shape[1] // 4
        piece = quarter // PIECES
        w_own = [
            lax.dynamic_slice_in_dim(
                out_weight, (2 * y + core) * quarter + k * piece, piece, 1
            )
            for k in range(PIECES)
        ]

    if kernels:
        both = jnp.concatenate([totals[0] * totals[1], totals[1]])
        both = jnp.pad(both, (0, STATE - 2 * heads_dev))
        high = both.astype(BF)
        low = (both - high.astype(F32)).astype(BF)
        gains = jnp.pad(jnp.stack([high, low]), ((0, HEAD_DIM // size - 2), (0, 0)))
        added = split_states(seq, code, totals, gains, own, per, size)
        added = exchange_states([after(v, *second) for v in added], seq, size)
        entered = entering_states(seq, conv_lengths, session_slots, cached_states, added)
        entered = exchange_states(entered, seq, size)
    else:
        one, two, code = plain_entering(
            seq, conv_lengths, session_slots, cached_states, totals, own, size
        )
        entered, second = [one], [two]
    where = seq if kernels else jnp.zeros_like(seq)
    if fast:
        weights = [lax.all_gather(part, "seq", axis=0) for part in w_own]
    gain = norm_gain.reshape(1, width)
    normed = [
        mix_groups(
            g, where, code, totals, x, z, b, c, by_group, by_row, step_t, gain, own, entered, second
        )
        for g in range(groups_dev)
    ]
    if not fast:
        return plain_projection(jnp.concatenate(normed, axis=1), out_weight)

    theirs, mine = 2 - 2 * head, 2 * head
    crossed = [lax.ppermute(part, "groups", SWAP) for part in normed]
    near = []
    for n, part in enumerate(normed):
        tied = after(part, *crossed[max(n - 2, 0) : n - 1]) if n > 1 else part
        near.append([part, lax.ppermute(tied, "batch", SWAP)])
    (near_others,) = project([theirs], near, weights[0], 1)
    (near_mine,) = project([mine], near, weights[0], 1)
    far = []
    for across in crossed:
        across = after(across, near_mine)
        far.append([across, lax.ppermute(across, "batch", SWAP)])
    far_others, far_mine = project([theirs, mine], far, weights[0], 2)
    lhs = [a + b for a, b in zip(near, far)]
    last = after(weights[1], far_mine)
    last_others = project([theirs], lhs, last, 2)
    last_mine = project([mine], lhs, after(last, *last_others), 2)
    sides = [
        in_order(y, core, to_rows([near_mine, far_mine], [near_others, far_others], tokens, True)),
        in_order(y, core, to_rows(last_mine, last_others, tokens, False)),
    ]
    pieces = [
        sides[k][q][:, block * piece : (block + 1) * piece]
        for block in range(2)
        for q in range(4)
        for k in range(PIECES)
    ]
    return jnp.concatenate(pieces, axis=1)[None]


def solution(mesh):
    placed = (
        P(("groups", "batch"), "seq", "head"),
        P(("groups", "batch"), "seq", "head"),
        P(("groups", "batch"), "seq", "head"),
        P(("groups", "batch"), "seq", "head"),
        P(("groups", "batch"), "seq", "head"),
        P(("groups", "batch"), "seq", "head"),
        P(("groups", "batch"), None, "head", "seq", None),
        P(("groups", "batch"), None),
        P(("groups", "batch"), None),
        P("head"),
        P("head", "seq"),
    )
    return jax.shard_map(
        body,
        mesh=mesh,
        in_specs=placed,
        out_specs=P(("groups", "batch"), "seq", "head"),
        check_vma=False,
    )
```
